512 devices in a mesh: dp: 64 (over x, z), tensor: 8 (over y, core).
Axes of the slice: x: 4, y: 4, z: 16, core: 2. Of those that a mesh axis runs over, the one named last changes fastest.
Arguments:
- responses: float32 [512, 6144], P('dp'), may hold values from -40 to 40
- weight: float32 [6144, 32768], P('dp', 'tensor'), may hold values from -1 to 1
- lengths: int32 [64], P('dp'), may hold values from 1 to 8, 256 in all
- targets: int32 [512], P('dp'), may hold values from 0 to 32767
- owners: int32 [64], P('dp'), may hold values from 0 to 63, each once
Outputs:
- logprobs: float32 [256], P('dp')
- grad_hidden: float32 [512, 6144], P('dp')
- grad_weight: float32 [6144, 32768], P('dp', 'tensor')
The draws below stay inside these ranges and needn't reach their ends.
Inputs may be any that keep to these rules, and one draw needn't show every extreme that they name: `lengths`: they sum to 256; the largest is 8. `owners`: each device index appears once.
All inputs are finite; a program needn't handle non-finite values. No bound on the sum of `lengths` on one device may be relied on, other than what follows from the above.
Results may differ from the reference program's by a relative error of at most 0.0003.
Values sent between devices are 32-bit elements; how exact they have to be, the bound alone decides.
No kernel may reach another device: no remote copies, remote signals or barrier semaphores. Data moves between devices by JAX's collectives and lax.ppermute only.
A program may use at most 64 MiB of HBM per device.

```python
import math
import jax
import jax.numpy as jnp
import numpy as np
from jax import lax

D = 6144
VOCAB = 32768
CAP = 8
TOTAL_ROWS = 256
N_DP = 64


def head_weight(key):
    key_base, key_scale, key_pair = jax.random.split(key, 3)
    base_draw = jax.random.normal(key_base, (D, VOCAB), jnp.float32)
    column_scale = jnp.exp(jax.random.uniform(key_scale, (VOCAB,), jnp.float32, math.log(0.5), math.log(5.0)))
    weight = base_draw * column_scale[None, :] / math.sqrt(D)
    pair_cols = 2 * jax.random.randint(key_pair, (16,), 0, VOCAB // 2)
    current = weight[:, pair_cols + 1]
    weight = weight.at[:, pair_cols + 1].set(current)
    return jnp.clip(weight, -1.0, 1.0)


def draw_weight(key, part):
    weight = head_weight(key)
    return weight


def draw_responses(key, part):
    slot_count = N_DP * CAP
    key_own = jax.random.fold_in(key, 7)
    key_vals, key_scale = jax.random.split(key_own, 2)
    row_scale = jnp.exp(jax.random.uniform(key_scale, (slot_count, 1), jnp.float32, math.log(0.3), math.log(3.0)))
    hidden = row_scale * jax.random.normal(key_vals, (slot_count, D), jnp.float32)
    return jnp.clip(hidden, -40.0, 40.0)


def set_ends(values, key, least, top_value):
    spot = [jax.random.randint(jax.random.fold_in(key, axis), (), 0, length) for axis, length in enumerate(values.shape)]
    main_axis = values.shape.index(max(values.shape))
    beside = spot[:main_axis] + [(spot[main_axis] + 1) % values.shape[main_axis]] + spot[main_axis + 1:]
    return values.at[tuple(spot)].set(least).at[tuple(beside)].set(top_value)


def rank_bounds(number_of, lean):
    weights = [(1 << 20) // math.isqrt(grade ** lean) + 1 for grade in range(1, number_of + 1)]
    deviation = 1 + sum(weights) // (1 << 30)
    return np.cumsum(np.array([max(1, weight // deviation) for weight in weights]))


def ranked_ids(stream_key, dims, number_of, lean):
    table = rank_bounds(number_of, lean)
    lot = jax.random.randint(jax.random.fold_in(stream_key, 1), dims, 0, int(table[number_of - 1]))
    rank = jnp.searchsorted(jnp.asarray(table, jnp.int32), lot, side="right")
    return jax.random.permutation(jax.random.fold_in(stream_key, 2), number_of)[rank].astype(jnp.int32)


def profile(amount, total, most, slope):
    loads = [(1 << 20) // math.isqrt(rank ** slope) + 1 for rank in range(2, amount + 1)]
    surplus, given = total - most - (amount - 1), [1] * (amount - 1)
    while surplus > 0:
        movable = [i for i in range(amount - 1) if given[i] < most]
        pool, remaining = sum([loads[i] for i in movable]), surplus
        for i in movable:
            more = min(most - given[i], max(1, remaining * loads[i] // pool), surplus)
            given[i] = given[i] + more
            surplus = surplus - more
    return np.array([most] + given)


def uneven_parts(stream_key, number_of, total, bound, slope):
    if number_of == 2:
        one = jax.random.randint(stream_key, (), max(1, total - bound), min(bound, total - 1) + 1)
        return jnp.stack([one, total - one])
    sizes = jnp.asarray(profile(number_of, total, bound, slope), jnp.int32)
    twos = (number_of - 1) // 2
    giver, taker = sizes[1:1 + 2 * twos:2], sizes[2:2 + 2 * twos:2]
    room = jnp.minimum(giver - 1, bound - taker)
    moved = jax.random.randint(jax.random.fold_in(stream_key, 1), (twos,), 0, 1 << 20) % (room + 1)
    sizes = sizes.at[1:1 + 2 * twos:2].set(giver - moved).at[2:2 + 2 * twos:2].set(taker + moved)
    return sizes[jax.random.permutation(jax.random.fold_in(stream_key, 2), number_of)]


def setup_inputs(seed: int = 0) -> dict:
    key_list = jax.random.split(jax.random.key(seed), 6)
    responses = draw_responses(jax.random.fold_in(key_list[5], 71), 0)
    weight = draw_weight(jax.random.fold_in(key_list[5], 71), 0)
    lengths = uneven_parts(key_list[2], N_DP, TOTAL_ROWS, CAP, 2).astype(jnp.int32)
    targets = set_ends(ranked_ids(key_list[3], (N_DP * CAP,), VOCAB, 2), jax.random.fold_in(key_list[3], 3), 0, VOCAB - 1).astype(jnp.int32)
    owners = jax.random.permutation(key_list[4], N_DP).astype(jnp.int32)
    return {"responses": responses, "weight": weight, "lengths": lengths, "targets": targets, "owners": owners}


HIGH = lax.Precision.HIGHEST


def live_rows(lengths):
    row_ends = jnp.cumsum(lengths).astype(jnp.int32)
    row_starts = (row_ends - lengths).astype(jnp.int32)
    row_ranks = jnp.arange(TOTAL_ROWS, dtype=jnp.int32)
    sources = jnp.sum((row_ends[None, :] <= row_ranks[:, None]).astype(jnp.int32), axis=1).astype(jnp.int32)
    slot_ids = (row_ranks - row_starts[sources]).astype(jnp.int32)
    return sources, slot_ids, (sources * CAP + slot_ids).astype(jnp.int32)


def reference(responses, weight, lengths, targets, owners):
    sources, slot_ids, positions = live_rows(lengths)
    hidden = responses[positions]
    labels = targets[positions]
    logits = jnp.dot(hidden, weight, precision=HIGH, preferred_element_type=jnp.float32)
    row_peak = jnp.max(logits, axis=1, keepdims=True)
    shifted = jnp.exp(logits - row_peak)
    exp_total = jnp.sum(shifted, axis=1, keepdims=True)
    onehot = (jnp.arange(VOCAB, dtype=jnp.int32)[None, :] == labels[:, None]).astype(jnp.float32)
    picked = jnp.sum(logits * onehot, axis=1)
    logprobs = picked - row_peak[:, 0] - jnp.log(exp_total[:, 0])
    grad_logits = onehot - shifted / exp_total
    grad_weight = jnp.dot(hidden.T, grad_logits, precision=HIGH, preferred_element_type=jnp.float32)
    grad_rows = jnp.dot(grad_logits, weight.T, precision=HIGH, preferred_element_type=jnp.float32)
    owner_rows = (owners[sources] * CAP + slot_ids).astype(jnp.int32)
    grad_hidden = jnp.zeros((N_DP * CAP, D), jnp.float32).at[owner_rows].set(grad_rows)
    return logprobs, grad_hidden, grad_weight
```

```python
import jax
import jax.numpy as jnp
from jax import lax
from jax.sharding import Mesh, PartitionSpec as P

HIGH = lax.Precision.HIGHEST
Z = ("h", "l")
XYC = ("x", "y", "c")
YC = ("y", "c")
META = 128


def swap(blocks, axes):
    return lax.all_to_all(blocks, axes, split_axis=0, concat_axis=0, tiled=True)


def spread(block, axes, count):
    return swap(jnp.broadcast_to(block[None], (count, *block.shape)), axes)


def shift_z(block, step):
    return lax.ppermute(block, Z, [(i, (i + step) % 16) for i in range(16)])


def dot(a, b, contract=(1, 0)):
    dims = (((contract[0],), (contract[1],)), ((), ()))
    return lax.dot_general(a, b, dims, precision=HIGH, preferred_element_type=jnp.float32)


def on_device(responses, weight, lengths, targets, owners):
    width = responses.shape[1]
    depth, columns = weight.shape
    quarter = columns // 4
    wide = 4 * depth
    x, h, l = lax.axis_index("x"), lax.axis_index("h"), lax.axis_index("l")
    j = lax.axis_index(YC)

    head = swap(weight.reshape(depth, 4, quarter).transpose(1, 0, 2), "x").reshape(wide, quarter)

    row = lax.dynamic_slice(responses, (j, 0), (1, width))
    row = row.reshape(4, 16, depth).transpose(1, 0, 2).reshape(16, wide)
    notes = jnp.stack([lax.dynamic_index_in_dim(targets, j, 0, False), lengths[0], owners[0]])
    notes = jnp.pad(notes.astype(jnp.float32), (0, META - 3))
    packed = jnp.concatenate([row, jnp.broadcast_to(notes[None], (16, META))], axis=1)
    mine = swap(packed[:, None, :], Z).reshape(16, wide + META)
    slots = spread(mine, XYC, 32).reshape(512, wide + META)

    ids = jnp.arange(512, dtype=jnp.int32)
    slot_j = (ids // 16) % 8
    source = (ids // 128) * 16 + ids % 16
    notes_all = slots[:, wide : wide + 3].astype(jnp.int32)
    slot_target, slot_length, slot_owner = notes_all[:, 0], notes_all[:, 1], notes_all[:, 2]
    before = (source[None, :] < source[:, None]) & (slot_j[None, :] == 0)
    starts = jnp.sum(jnp.where(before, slot_length[None, :], 0), axis=1)
    live = slot_j < slot_length
    rank = jnp.where(live, (starts + slot_j - 64 * l) % 256, -1)
    rows = jnp.arange(256, dtype=jnp.int32)
    select = rank[None, :] == rows[:, None]
    hidden = dot(select.astype(jnp.float32), slots[:, :wide])
    labels = jnp.sum(jnp.where(select, slot_target[None, :], 0), axis=1)
    owned = (slot_owner[None, :] == source[:, None]) & (slot_j[None, :] == slot_j[:, None])
    sent_rank = jnp.sum(jnp.where(owned, rank[None, :] + 1, 0), axis=1) - 1
    deliver = (sent_rank[:, None] == rows[None, :]).astype(jnp.float32)

    partial = dot(hidden, head)
    up = shift_z(partial[64:128], 1)
    down = shift_z(partial[192:256], -1)
    up2 = shift_z(partial[128:160], 2)
    down2 = shift_z(partial[160:192], -2)
    block = partial[:64] + up + down + jnp.concatenate([up2, down2], axis=0)
    logits = jnp.sum(swap(block.reshape(4, 16, quarter), "h"), axis=0)

    row_labels = lax.dynamic_slice(labels, (h * 16,), (16,))
    column = jnp.arange(quarter, dtype=jnp.int32) + j * columns + x * quarter
    onehot = (column[None, :] == row_labels[:, None]).astype(jnp.float32)
    peak = jnp.max(logits, axis=1)
    shifted = jnp.exp(logits - peak[:, None])
    stats = jnp.stack([peak, jnp.sum(shifted, axis=1), jnp.sum(logits * onehot, axis=1)], axis=0)
    stats = spread(stats, XYC, 32)
    row_peak = jnp.max(stats[:, 0], axis=0)
    exp_total = jnp.sum(stats[:, 1] * jnp.exp(stats[:, 0] - row_peak[None]), axis=0)
    logprobs = jnp.sum(stats[:, 2], axis=0) - row_peak - jnp.log(exp_total)
    scale = jnp.exp(peak - row_peak) / exp_total
    grad = onehot - shifted * scale[:, None]

    own = spread(grad, "h", 4).reshape(64, quarter)
    after = shift_z(own, -1)
    ahead = shift_z(own, 1)
    far = shift_z(own[:32], 2)
    far2 = shift_z(own[32:], -2)
    grads = jnp.concatenate([own, after, far, far2, ahead], axis=0)

    grad_head = dot(hidden, grads, (0, 0)).reshape(4, depth, quarter)
    grad_weight = swap(grad_head, "x").transpose(1, 0, 2).reshape(depth, columns)

    grad_rows = dot(grads, head, (1, 1))
    leaving = dot(deliver, grad_rows).reshape(32, 16, wide)
    summed = jnp.sum(swap(leaving, XYC), axis=0)
    parts = lax.dynamic_update_slice(jnp.zeros((16, META), jnp.float32), logprobs.reshape(4, 4), (h * 4, 0))
    parts = jnp.where(l == x, parts, 0.0)
    arrived = swap(jnp.concatenate([summed, parts], axis=1)[:, None, :], Z)[:, 0]
    slot = arrived[:, :wide].reshape(16, 4, depth).transpose(1, 0, 2).reshape(width)
    grad_hidden = spread(slot, YC, 8)
    return jnp.sum(arrived[:, wide : wide + 4], axis=0), grad_hidden, grad_weight


def solution(mesh):
    grid = Mesh(mesh.devices.reshape(4, 4, 4, 4, 2), ("x", "h", "l", "y", "c"))
    dp = ("x", "h", "l")
    placed = (P(dp, None), P(dp, YC), P(dp), P(dp), P(dp))
    return jax.shard_map(
        on_device,
        mesh=grid,
        in_specs=placed,
        out_specs=(P(dp), P(dp, None), P(dp, YC)),
        check_vma=False,
    )
```

```python
import jax
import jax.numpy as jnp
from jax import lax
from jax.sharding import Mesh, PartitionSpec as P

HIGH = lax.Precision.HIGHEST
Z = ("h", "l")
XYC = ("x", "y", "c")
YC = ("y", "c")
META = 128


def swap(blocks, axes):
    return lax.all_to_all(blocks, axes, split_axis=0, concat_axis=0, tiled=True)


def spread(block, axes, count):
    return swap(jnp.broadcast_to(block[None], (count, *block.shape)), axes)


def shift_z(block, step):
    return lax.ppermute(block, Z, [(i, (i + step) % 16) for i in range(16)])


def shift_x(block, step):
    return lax.ppermute(block, "x", [(i, (i + step) % 4) for i in range(4)])


def turn(block, chip):
    depth = block.shape[-1] // 4
    order = [(chip - s) % 4 for s in range(4)]
    return jnp.concatenate([block[..., depth * i : depth * (i + 1)] for i in order], axis=-1)


def dot(a, b, contract=(1, 0)):
    dims = (((contract[0],), (contract[1],)), ((), ()))
    return lax.dot_general(a, b, dims, precision=HIGH, preferred_element_type=jnp.float32)


def on_device(responses, weight, lengths, targets, owners):
    width = responses.shape[1]
    depth, columns = weight.shape
    quarter = columns // 4
    wide = 4 * depth
    x, h, l = lax.axis_index("x"), lax.axis_index("h"), lax.axis_index("l")
    j = lax.axis_index(YC)

    heads = [
        shift_x(lax.dynamic_slice(weight, (0, (x + s) % 4 * quarter), (depth, quarter)), s) if s
        else lax.dynamic_slice(weight, (0, x * quarter), (depth, quarter))
        for s in range(4)
    ]

    row = lax.dynamic_slice(responses, (j, 0), (1, width))
    row = row.reshape(4, 16, depth).transpose(1, 0, 2).reshape(16, wide)
    notes = jnp.stack([lax.dynamic_index_in_dim(targets, j, 0, False), lengths[0], owners[0]])
    notes = jnp.pad(notes.astype(jnp.float32), (0, META - 3))
    packed = jnp.concatenate([row, jnp.broadcast_to(notes[None], (16, META))], axis=1)
    mine = swap(packed[:, None, :], Z).reshape(16, wide + META)
    turned = jnp.stack([jnp.concatenate([turn(mine[:, :wide], i), mine[:, wide:]], axis=1) for i in range(4)])
    copies = jnp.broadcast_to(turned[:, None], (4, 8, 16, wide + META)).reshape(32, 16, wide + META)
    slots = swap(copies, XYC).reshape(512, wide + META)

    ids = jnp.arange(512, dtype=jnp.int32)
    slot_j = (ids // 16) % 8
    source = (ids // 128) * 16 + ids % 16
    notes_all = slots[:, wide : wide + 3].astype(jnp.int32)
    slot_target, slot_length, slot_owner = notes_all[:, 0], notes_all[:, 1], notes_all[:, 2]
    before = (source[None, :] < source[:, None]) & (slot_j[None, :] == 0)
    starts = jnp.sum(jnp.where(before, slot_length[None, :], 0), axis=1)
    live = slot_j < slot_length
    rank = jnp.where(live, (starts + slot_j - 64 * l) % 256, -1)
    rows = jnp.arange(256, dtype=jnp.int32)
    select = rank[None, :] == rows[:, None]
    hidden = dot(select.astype(jnp.float32), slots[:, :wide])
    labels = jnp.sum(jnp.where(select, slot_target[None, :], 0), axis=1)
    owned = (slot_owner[None, :] == source[:, None]) & (slot_j[None, :] == slot_j[:, None])
    sent_rank = jnp.sum(jnp.where(owned, rank[None, :] + 1, 0), axis=1) - 1
    deliver = (sent_rank[:, None] == rows[None, :]).astype(jnp.float32)

    head = jnp.concatenate(heads, axis=0)
    partial = dot(hidden, head)
    up = shift_z(partial[64:128], 1)
    down = shift_z(partial[192:256], -1)
    up2 = shift_z(partial[128:160], 2)
    down2 = shift_z(partial[160:192], -2)
    block = partial[:64] + up + down + jnp.concatenate([up2, down2], axis=0)
    logits = jnp.sum(swap(block.reshape(4, 16, quarter), "h"), axis=0)

    row_labels = lax.dynamic_slice(labels, (h * 16,), (16,))
    column = jnp.arange(quarter, dtype=jnp.int32) + j * columns + x * quarter
    onehot = (column[None, :] == row_labels[:, None]).astype(jnp.float32)
    peak = jnp.max(logits, axis=1)
    shifted = jnp.exp(logits - peak[:, None])
    stats = jnp.stack([peak, jnp.sum(shifted, axis=1), jnp.sum(logits * onehot, axis=1)], axis=0)
    stats = spread(stats, XYC, 32)
    row_peak = jnp.max(stats[:, 0], axis=0)
    exp_total = jnp.sum(stats[:, 1] * jnp.exp(stats[:, 0] - row_peak[None]), axis=0)
    logprobs = jnp.sum(stats[:, 2], axis=0) - row_peak - jnp.log(exp_total)
    scale = jnp.exp(peak - row_peak) / exp_total
    grad = onehot - shifted * scale[:, None]

    own = spread(grad, "h", 4).reshape(64, quarter)
    after = shift_z(own, -1)
    ahead = shift_z(own, 1)
    far = shift_z(own[:32], 2)
    far2 = shift_z(own[32:], -2)
    grads = jnp.concatenate([own, after, far, far2, ahead], axis=0)

    grad_head = dot(hidden, grads, (0, 0)).reshape(4, depth, quarter)
    grad_weight = jnp.zeros((depth, columns), jnp.float32)
    for s in range(4):
        part = shift_x(grad_head[s], -s) if s else grad_head[0]
        grad_weight = lax.dynamic_update_slice(grad_weight, part, (0, (x + s) % 4 * quarter))

    grad_rows = dot(grads, head, (1, 1))
    leaving = dot(deliver, grad_rows).reshape(32, 16, wide)
    summed = jnp.sum(swap(leaving, XYC).reshape(4, 8, 16, wide), axis=1)
    summed = sum(turn(summed[i], i) for i in range(4))
    parts = lax.dynamic_update_slice(jnp.zeros((16, META), jnp.float32), logprobs.reshape(4, 4), (h * 4, 0))
    parts = jnp.where(l == x, parts, 0.0)
    arrived = swap(jnp.concatenate([summed, parts], axis=1)[:, None, :], Z)[:, 0]
    slot = arrived[:, :wide].reshape(16, 4, depth).transpose(1, 0, 2).reshape(width)
    grad_hidden = spread(slot, YC, 8)
    return jnp.sum(arrived[:, wide : wide + 4], axis=0), grad_hidden, grad_weight


def solution(mesh):
    grid = Mesh(mesh.devices.reshape(4, 4, 4, 4, 2), ("x", "h", "l", "y", "c"))
    dp = ("x", "h", "l")
    placed = (P(dp, None), P(dp, YC), P(dp), P(dp), P(dp))
    return jax.shard_map(
        on_device,
        mesh=grid,
        in_specs=placed,
        out_specs=(P(dp), P(dp, None), P(dp, YC)),
        check_vma=False,
    )
```

```python
import jax
import jax.numpy as jnp
from jax import lax
from jax.sharding import Mesh, PartitionSpec as P

HIGH = lax.Precision.HIGHEST
Z = ("h", "l")
XYC = ("x", "y", "c")
YC = ("y", "c")
META = 128


def swap(blocks, axes):
    return lax.all_to_all(blocks, axes, split_axis=0, concat_axis=0, tiled=True)


def spread(block, axes, count):
    return swap(jnp.broadcast_to(block[None], (count, *block.shape)), axes)


def shift_z(block, step):
    return lax.ppermute(block, Z, [(i, (i + step) % 16) for i in range(16)])


def shift_far(block):
    pairs = [(2 * i + c, 2 * ((i + 2 - 4 * c) % 16) + c) for i in range(16) for c in range(2)]
    return lax.ppermute(block, ("h", "l", "c"), pairs)


def shift_x(block, step):
    return lax.ppermute(block, "x", [(i, (i + step) % 4) for i in range(4)])


def turn(block, chip):
    depth = block.shape[-1] // 4
    order = [(chip - s) % 4 for s in range(4)]
    return jnp.concatenate([block[..., depth * i : depth * (i + 1)] for i in order], axis=-1)


def dot(a, b, contract=(1, 0)):
    dims = (((contract[0],), (contract[1],)), ((), ()))
    return lax.dot_general(a, b, dims, precision=HIGH, preferred_element_type=jnp.float32)


def on_device(responses, weight, lengths, targets, owners):
    width = responses.shape[1]
    depth, columns = weight.shape
    quarter = columns // 4
    wide = 4 * depth
    x, h, l = lax.axis_index("x"), lax.axis_index("h"), lax.axis_index("l")
    j = lax.axis_index(YC)

    heads = [
        shift_x(lax.dynamic_slice(weight, (0, (x + s) % 4 * quarter), (depth, quarter)), s) if s
        else lax.dynamic_slice(weight, (0, x * quarter), (depth, quarter))
        for s in range(4)
    ]

    row = lax.dynamic_slice(responses, (j, 0), (1, width))
    row = row.reshape(4, 16, depth).transpose(1, 0, 2).reshape(16, wide)
    notes = jnp.stack([lax.dynamic_index_in_dim(targets, j, 0, False), lengths[0], owners[0]])
    notes = jnp.pad(notes.astype(jnp.float32), (0, META - 3))
    packed = jnp.concatenate([row, jnp.broadcast_to(notes[None], (16, META))], axis=1)
    mine = swap(packed[:, None, :], Z).reshape(16, wide + META)
    turned = jnp.stack([jnp.concatenate([turn(mine[:, :wide], i), mine[:, wide:]], axis=1) for i in range(4)])
    turned, *heads = lax.optimization_barrier((turned, *heads))
    copies = jnp.broadcast_to(turned[:, None], (4, 8, 16, wide + META)).reshape(32, 16, wide + META)
    slots = swap(copies, XYC).reshape(512, wide + META)

    ids = jnp.arange(512, dtype=jnp.int32)
    slot_j = (ids // 16) % 8
    source = (ids // 128) * 16 + ids % 16
    notes_all = slots[:, wide : wide + 3].astype(jnp.int32)
    slot_target, slot_length, slot_owner = notes_all[:, 0], notes_all[:, 1], notes_all[:, 2]
    before = (source[None, :] < source[:, None]) & (slot_j[None, :] == 0)
    starts = jnp.sum(jnp.where(before, slot_length[None, :], 0), axis=1)
    live = slot_j < slot_length
    rank = jnp.where(live, (starts + slot_j - 64 * l) % 256, -1)
    rows = jnp.arange(256, dtype=jnp.int32)
    select = rank[None, :] == rows[:, None]
    hidden = dot(select.astype(jnp.float32), slots[:, :wide])
    labels = jnp.sum(jnp.where(select, slot_target[None, :], 0), axis=1)
    owned = (slot_owner[None, :] == source[:, None]) & (slot_j[None, :] == slot_j[:, None])
    sent_rank = jnp.sum(jnp.where(owned, rank[None, :] + 1, 0), axis=1) - 1
    deliver = (sent_rank[:, None] == rows[None, :]).astype(jnp.float32)

    head = jnp.concatenate(heads, axis=0)
    partial = dot(hidden, head)
    up = shift_z(partial[64:128], 1)
    down = shift_z(partial[192:256], -1)
    block = partial[:64] + up + down + shift_far(partial[128:192])
    logits = jnp.sum(swap(block.reshape(4, 16, quarter), "h"), axis=0)

    row_labels = lax.dynamic_slice(labels, (h * 16,), (16,))
    column = jnp.arange(quarter, dtype=jnp.int32) + j * columns + x * quarter
    onehot = (column[None, :] == row_labels[:, None]).astype(jnp.float32)
    peak = jnp.max(logits, axis=1)
    shifted = jnp.exp(logits - peak[:, None])
    stats = jnp.stack([peak, jnp.sum(shifted, axis=1), jnp.sum(logits * onehot, axis=1)], axis=0)
    stats = spread(stats, XYC, 32)
    row_peak = jnp.max(stats[:, 0], axis=0)
    exp_total = jnp.sum(stats[:, 1] * jnp.exp(stats[:, 0] - row_peak[None]), axis=0)
    logprobs = jnp.sum(stats[:, 2], axis=0) - row_peak - jnp.log(exp_total)
    scale = jnp.exp(peak - row_peak) / exp_total
    grad = onehot - shifted * scale[:, None]

    own = spread(grad, "h", 4).reshape(64, quarter)
    after = shift_z(own, -1)
    ahead = shift_z(own, 1)
    grads = jnp.concatenate([own, after, shift_far(own), ahead], axis=0)

    grad_head = dot(hidden, grads, (0, 0)).reshape(4, depth, quarter)
    grad_weight = jnp.zeros((depth, columns), jnp.float32)
    for s in range(4):
        part = shift_x(grad_head[s], -s) if s else grad_head[0]
        grad_weight = lax.dynamic_update_slice(grad_weight, part, (0, (x + s) % 4 * quarter))

    grad_rows = dot(grads, head, (1, 1))
    leaving = dot(deliver, grad_rows).reshape(32, 16, wide)
    summed = jnp.sum(swap(leaving, XYC).reshape(4, 8, 16, wide), axis=1)
    summed = sum(turn(summed[i], i) for i in range(4))
    parts = lax.dynamic_update_slice(jnp.zeros((16, META), jnp.float32), logprobs.reshape(4, 4), (h * 4, 0))
    parts = jnp.where(l == x, parts, 0.0)
    arrived = swap(jnp.concatenate([summed, parts], axis=1)[:, None, :], Z)[:, 0]
    slot = arrived[:, :wide].reshape(16, 4, depth).transpose(1, 0, 2).reshape(width)
    grad_hidden = spread(slot, YC, 8)
    return jnp.sum(arrived[:, wide : wide + 4], axis=0), grad_hidden, grad_weight


def solution(mesh):
    grid = Mesh(mesh.devices.reshape(4, 4, 4, 4, 2), ("x", "h", "l", "y", "c"))
    dp = ("x", "h", "l")
    placed = (P(dp, None), P(dp, YC), P(dp), P(dp), P(dp))
    return jax.shard_map(
        on_device,
        mesh=grid,
        in_specs=placed,
        out_specs=(P(dp), P(dp, None), P(dp, YC)),
        check_vma=False,
    )
```

```python
import jax
import jax.numpy as jnp
from jax import lax
from jax.sharding import Mesh, PartitionSpec as P

HIGH = lax.Precision.HIGHEST
Z = ("h", "l")
XYC = ("x", "y", "c")
LYC = ("l", "y", "c")
YC = ("y", "c")
META = 128


def swap(blocks, axes):
    return lax.all_to_all(blocks, axes, split_axis=0, concat_axis=0, tiled=True)


def spread(block, axes, count):
    return swap(jnp.broadcast_to(block[None], (count, *block.shape)), axes)


def shift_z(block, step):
    return lax.ppermute(block, Z, [(i, (i + step) % 16) for i in range(16)])


def shift_far(block, sign):
    step = [2 * sign, -2 * sign]
    pairs = [(2 * i + c, 2 * ((i + step[c]) % 16) + c) for i in range(16) for c in range(2)]
    return lax.ppermute(block, ("h", "l", "c"), pairs)


def dot(a, b, contract=(1, 0)):
    dims = (((contract[0],), (contract[1],)), ((), ()))
    return lax.dot_general(a, b, dims, precision=HIGH, preferred_element_type=jnp.float32)


def on_device(responses, weight, lengths, targets, owners):
    width = responses.shape[1]
    depth, columns = weight.shape
    quarter = columns // 4
    wide = 4 * depth
    x, h, l = lax.axis_index("x"), lax.axis_index("h"), lax.axis_index("l")
    j = lax.axis_index(YC)

    def cut(s):
        return lax.dynamic_slice(weight, (0, (l + s) % 4 * quarter), (depth, quarter))

    head = jnp.concatenate([shift_z(cut(1), 1), cut(0), shift_z(cut(3), -1), shift_far(cut(2), 1)], axis=0)

    row = lax.dynamic_slice(responses, (j, 0), (1, width)).reshape(4, 16, depth)
    near = jnp.concatenate([jnp.roll(row, -d, axis=1) for d in range(-2, 3)], axis=2)
    notes = jnp.stack([lax.dynamic_index_in_dim(targets, j, 0, False), lengths[0], owners[0]])
    notes = jnp.pad(notes.astype(jnp.float32), (0, META - 3))
    packed = jnp.concatenate(
        [near.transpose(1, 0, 2).reshape(16, 20 * depth), jnp.broadcast_to(notes[None], (16, META))], axis=1
    )
    mine = swap(packed[:, None, :], Z).reshape(16, 20 * depth + META)
    chunks = []
    for i in range(4):
        base = mine[:, 5 * depth * i : 5 * depth * (i + 1)]
        chunks.append(jnp.concatenate([base[:, depth : 4 * depth], base[:, :depth], mine[:, 20 * depth :]], axis=1))
        chunks.append(jnp.concatenate([base[:, depth:], mine[:, 20 * depth :]], axis=1))
    chunks = jnp.stack(chunks).reshape(4, 1, 2, 16, wide + META)
    copies = jnp.broadcast_to(chunks, (4, 4, 2, 16, wide + META)).reshape(32, 16, wide + META)
    slots = swap(copies, XYC).reshape(512, wide + META)

    ids = jnp.arange(512, dtype=jnp.int32)
    slot_j = (ids // 16) % 8
    source = (ids // 128) * 16 + ids % 16
    notes_all = slots[:, wide : wide + 3].astype(jnp.int32)
    slot_target, slot_length, slot_owner = notes_all[:, 0], notes_all[:, 1], notes_all[:, 2]
    before = (source[None, :] < source[:, None]) & (slot_j[None, :] == 0)
    starts = jnp.sum(jnp.where(before, slot_length[None, :], 0), axis=1)
    rank = jnp.where(slot_j < slot_length, starts + slot_j, -1)
    rows = jnp.arange(256, dtype=jnp.int32)
    select = rank[None, :] == rows[:, None]
    hidden = dot(select.astype(jnp.float32), slots[:, :wide])
    labels = jnp.sum(jnp.where(select, slot_target[None, :], 0), axis=1)
    owned = (slot_owner[None, :] == source[:, None]) & (slot_j[None, :] == slot_j[:, None])
    sent_rank = jnp.sum(jnp.where(owned, rank[None, :] + 1, 0), axis=1) - 1
    deliver = (sent_rank[:, None] == rows[None, :]).astype(jnp.float32)

    partial = dot(hidden, head)
    block = jnp.sum(swap(partial.reshape(4, 64, quarter), "x"), axis=0)
    logits = jnp.sum(swap(block.reshape(4, 16, quarter), "h"), axis=0)

    row_labels = lax.dynamic_slice(labels, (x * 64 + h * 16,), (16,))
    column = jnp.arange(quarter, dtype=jnp.int32) + j * columns + l * quarter
    onehot = (column[None, :] == row_labels[:, None]).astype(jnp.float32)
    peak = jnp.max(logits, axis=1)
    shifted = jnp.exp(logits - peak[:, None])
    stats = jnp.stack([peak, jnp.sum(shifted, axis=1), jnp.sum(logits * onehot, axis=1)], axis=0)
    stats = spread(stats, LYC, 32)
    row_peak = jnp.max(stats[:, 0], axis=0)
    exp_total = jnp.sum(stats[:, 1] * jnp.exp(stats[:, 0] - row_peak[None]), axis=0)
    logprobs = jnp.sum(stats[:, 2], axis=0) - row_peak - jnp.log(exp_total)
    scale = jnp.exp(peak - row_peak) / exp_total
    grad = onehot - shifted * scale[:, None]

    grads = spread(spread(grad, "h", 4).reshape(64, quarter), "x", 4).reshape(256, quarter)

    grad_head = dot(hidden, grads, (0, 0)).reshape(4, depth, quarter)
    grad_weight = jnp.zeros((depth, columns), jnp.float32)
    back = [grad_head[1], shift_z(grad_head[0], -1), shift_far(grad_head[3], -1), shift_z(grad_head[2], 1)]
    for s in range(4):
        grad_weight = lax.dynamic_update_slice(grad_weight, back[s], (0, (l + s) % 4 * quarter))

    grad_rows = dot(grads, head, (1, 1))
    leaving = dot(deliver, grad_rows).reshape(32, 16, wide)
    summed = jnp.sum(swap(leaving, XYC).reshape(4, 4, 2, 16, wide), axis=1)
    even, odd = summed[:, 0], summed[:, 1]
    near = jnp.concatenate(
        [even[..., 3 * depth :], even[..., : 3 * depth] + odd[..., : 3 * depth], odd[..., 3 * depth :]], axis=-1
    )
    near = near.transpose(1, 0, 2).reshape(16, 1, 20 * depth)
    arrived = swap(near, Z).reshape(16, 4, 5, depth)
    slot = sum(jnp.roll(arrived[:, :, d + 2], d, axis=0) for d in range(-2, 3))
    grad_hidden = spread(slot.transpose(1, 0, 2).reshape(width), YC, 8)
    return lax.dynamic_slice(logprobs, (4 * l,), (4,)), grad_hidden, grad_weight


def solution(mesh):
    grid = Mesh(mesh.devices.reshape(4, 4, 4, 4, 2), ("x", "h", "l", "y", "c"))
    dp = ("x", "h", "l")
    placed = (P(dp, None), P(dp, YC), P(dp), P(dp), P(dp))
    return jax.shard_map(
        on_device,
        mesh=grid,
        in_specs=placed,
        out_specs=(P(dp), P(dp, None), P(dp, YC)),
        check_vma=False,
    )
```

```python
import jax
import jax.numpy as jnp
from jax import lax
from jax.sharding import Mesh, PartitionSpec as P

HIGH = lax.Precision.HIGHEST
Z = ("h", "l")
XYC = ("x", "y", "c")
LYC = ("l", "y", "c")
YC = ("y", "c")
GRAD = lax.Precision.HIGH


def swap(blocks, axes):
    return lax.all_to_all(blocks, axes, split_axis=0, concat_axis=0, tiled=True)


def spread(block, axes, count):
    return swap(jnp.broadcast_to(block[None], (count, *block.shape)), axes)


def shift_z(block, step):
    return lax.ppermute(block, Z, [(i, (i + step) % 16) for i in range(16)])


def shift_far(block, sign):
    step = [2 * sign, -2 * sign]
    pairs = [(2 * i + c, 2 * ((i + step[c]) % 16) + c) for i in range(16) for c in range(2)]
    return lax.ppermute(block, ("h", "l", "c"), pairs)


def dot(a, b, contract=(1, 0), precision=HIGH):
    dims = (((contract[0],), (contract[1],)), ((), ()))
    return lax.dot_general(a, b, dims, precision=precision, preferred_element_type=jnp.float32)


def on_device(responses, weight, lengths, targets, owners):
    width = responses.shape[1]
    depth, columns = weight.shape
    quarter = columns // 4
    wide = 4 * depth
    packed_wide = 128 * ((5 * depth + 10 + 127) // 128)
    x, h, l = lax.axis_index("x"), lax.axis_index("h"), lax.axis_index("l")
    j, c = lax.axis_index(YC), lax.axis_index("c")

    def cut(s):
        return lax.dynamic_slice(weight, (0, (l + s) % 4 * quarter), (depth, quarter))

    below, above, far = shift_z(cut(1), 1), shift_z(cut(3), -1), shift_far(cut(2), 1)

    row = lax.dynamic_slice(responses, (j, 0), (1, width)).reshape(4, 16, depth)
    notes = jnp.concatenate([targets, lengths, owners]).astype(jnp.float32)
    notes = jnp.broadcast_to(jnp.pad(notes, (0, packed_wide - 5 * depth - 10)), (4, 16, packed_wide - 5 * depth))
    near = jnp.concatenate([*(jnp.roll(row, -d, axis=1) for d in range(-2, 3)), notes], axis=2)
    mine = swap(near.transpose(1, 0, 2).reshape(16, 1, 4 * packed_wide), Z)
    chunks = mine.reshape(16, 4, packed_wide).transpose(1, 0, 2)
    chunks, below = lax.optimization_barrier((chunks, below))
    copies = jnp.broadcast_to(chunks[:, None], (4, 8, 16, packed_wide)).reshape(32, 16, packed_wide)
    slots = swap(copies, XYC).reshape(512, packed_wide)

    ids = jnp.arange(512, dtype=jnp.int32)
    slot_j = (ids // 16) % 8
    source = (ids // 128) * 16 + ids % 16
    notes_all = slots[:, 5 * depth : 5 * depth + 10].astype(jnp.int32)
    slot_length, slot_owner = notes_all[:, 8], notes_all[:, 9]
    slot_target = jnp.sum(jnp.where(jnp.arange(10)[None, :] == slot_j[:, None], notes_all, 0), axis=1)
    before = (source[None, :] < source[:, None]) & (slot_j[None, :] == 0)
    starts = jnp.sum(jnp.where(before, slot_length[None, :], 0), axis=1)
    rank = jnp.where(slot_j < slot_length, starts + slot_j, -1)
    rows = jnp.arange(256, dtype=jnp.int32)
    select = rank[None, :] == rows[:, None]
    hidden = dot(select.astype(jnp.float32), slots[:, : 5 * depth])
    labels = jnp.sum(jnp.where(select, slot_target[None, :], 0), axis=1)
    owned = (slot_owner[None, :] == source[:, None]) & (slot_j[None, :] == slot_j[:, None])
    sent_rank = jnp.sum(jnp.where(owned, rank[None, :] + 1, 0), axis=1) - 1
    deliver = (sent_rank[:, None] == rows[None, :]).astype(jnp.float32)

    none = jnp.zeros_like(far)
    head = jnp.concatenate([jnp.where(c == 0, far, none), below, cut(0), above, jnp.where(c == 0, none, far)], axis=0)
    head = lax.optimization_barrier(head)

    partial = dot(hidden, head)
    block = jnp.sum(swap(partial.reshape(4, 64, quarter), "x"), axis=0)
    logits = jnp.sum(swap(block.reshape(4, 16, quarter), "h"), axis=0)

    row_labels = lax.dynamic_slice(labels, (x * 64 + h * 16,), (16,))
    column = jnp.arange(quarter, dtype=jnp.int32) + j * columns + l * quarter
    onehot = (column[None, :] == row_labels[:, None]).astype(jnp.float32)
    peak = jnp.max(logits, axis=1)
    shifted = jnp.exp(logits - peak[:, None])
    stats = jnp.stack([peak, jnp.sum(shifted, axis=1), jnp.sum(logits * onehot, axis=1)], axis=0)
    stats = spread(stats, LYC, 32)
    row_peak = jnp.max(stats[:, 0], axis=0)
    exp_total = jnp.sum(stats[:, 1] * jnp.exp(stats[:, 0] - row_peak[None]), axis=0)
    logprobs = jnp.sum(stats[:, 2], axis=0) - row_peak - jnp.log(exp_total)
    scale = jnp.exp(peak - row_peak) / exp_total
    grad = onehot - shifted * scale[:, None]

    grads = spread(spread(grad, "h", 4).reshape(64, quarter), "x", 4).reshape(256, quarter)

    grad_head = dot(hidden, grads, (0, 0), GRAD).reshape(5, depth, quarter)
    far = shift_far(jnp.where(c == 0, grad_head[0], grad_head[4]), -1)
    above, below = shift_z(grad_head[1], -1), shift_z(grad_head[3], 1)

    grad_rows = dot(grads, head, (1, 1), GRAD)
    grad_rows = jnp.where(c == 0, grad_rows[:, :wide], grad_rows[:, depth:])
    leaving = dot(deliver, grad_rows, (1, 0), GRAD).reshape(32, 16, wide)
    summed = jnp.sum(swap(leaving, XYC).reshape(4, 4, 2, 16, wide), axis=1)
    near = jnp.pad(summed[:, 0], ((0, 0), (0, 0), (0, depth))) + jnp.pad(summed[:, 1], ((0, 0), (0, 0), (depth, 0)))
    near = near.transpose(1, 0, 2).reshape(16, 1, 20 * depth)
    near, above, below = lax.optimization_barrier((near, above, below))
    arrived = swap(near, Z).reshape(16, 4, 5, depth)
    slot = sum(jnp.roll(arrived[:, :, d + 2], d, axis=0) for d in range(-2, 3))
    grad_weight = jnp.zeros((depth, columns), jnp.float32)
    for s, part in enumerate((grad_head[2], above, far, below)):
        grad_weight = lax.dynamic_update_slice(grad_weight, part, (0, (l + s) % 4 * quarter))
    grad_hidden = spread(slot.transpose(1, 0, 2).reshape(width), YC, 8)
    return lax.dynamic_slice(logprobs, (4 * l,), (4,)), grad_hidden, grad_weight


def solution(mesh):
    grid = Mesh(mesh.devices.reshape(4, 4, 4, 4, 2), ("x", "h", "l", "y", "c"))
    dp = ("x", "h", "l")
    placed = (P(dp, None), P(dp, YC), P(dp), P(dp), P(dp))
    return jax.shard_map(
        on_device,
        mesh=grid,
        in_specs=placed,
        out_specs=(P(dp), P(dp, None), P(dp, YC)),
        check_vma=False,
    )
```

```python
import jax
import jax.numpy as jnp
from jax import lax
from jax.sharding import Mesh, PartitionSpec as P

HIGH = lax.Precision.HIGHEST
GRAD = lax.Precision.HIGH
Z = ("h", "l")
XYC = ("x", "y", "c")
YC = ("y", "c")
META = 128


def swap(blocks, axes):
    return lax.all_to_all(blocks, axes, split_axis=0, concat_axis=0, tiled=True)


def spread(block, axes, count):
    return swap(jnp.broadcast_to(block[None], (count, *block.shape)), axes)


def shift_z(block, step):
    return lax.ppermute(block, Z, [(i, (i + step) % 16) for i in range(16)])


def shift_far(block):
    pairs = [(2 * i + c, 2 * ((i + 2 - 4 * c) % 16) + c) for i in range(16) for c in range(2)]
    return lax.ppermute(block, ("h", "l", "c"), pairs)


def shift_x(block, step):
    return lax.ppermute(block, "x", [(i, (i + step) % 4) for i in range(4)])


def dot(a, b, contract=(1, 0), precision=HIGH):
    dims = (((contract[0],), (contract[1],)), ((), ()))
    return lax.dot_general(a, b, dims, precision=precision, preferred_element_type=jnp.float32)


def on_device(responses, weight, lengths, targets, owners):
    width = responses.shape[1]
    depth, columns = weight.shape
    quarter = columns // 4
    wide = 4 * depth
    x, h, l = lax.axis_index("x"), lax.axis_index("h"), lax.axis_index("l")
    j = lax.axis_index(YC)

    def cut(s):
        return lax.dynamic_slice(weight, (0, (x + s) % 4 * quarter), (depth, quarter))

    pieces = [cut(0), *(shift_x(cut(s), s) for s in range(1, 4))]

    row = lax.dynamic_slice(responses, (j, 0), (1, width)).reshape(4, 16, depth)
    notes = jnp.pad(jnp.concatenate([targets, lengths, owners]).astype(jnp.float32), (0, META - 10))
    notes = jnp.broadcast_to(notes, (16, META))
    packed = jnp.concatenate([row.transpose(1, 0, 2).reshape(16, wide), notes], axis=1)
    mine = swap(packed.reshape(16, 1, wide + META), Z).reshape(16, wide + META)
    mine, pieces[1] = lax.optimization_barrier((mine, pieces[1]))
    slots = spread(mine, XYC, 32).reshape(512, wide + META)

    ids = jnp.arange(512, dtype=jnp.int32)
    slot_j = (ids // 16) % 8
    source = (ids // 128) * 16 + ids % 16
    notes_all = slots[:, wide : wide + 10].astype(jnp.int32)
    slot_length, slot_owner = notes_all[:, 8], notes_all[:, 9]
    slot_target = jnp.sum(jnp.where(jnp.arange(10)[None, :] == slot_j[:, None], notes_all, 0), axis=1)
    before = (source[None, :] < source[:, None]) & (slot_j[None, :] == 0)
    starts = jnp.sum(jnp.where(before, slot_length[None, :], 0), axis=1)
    rank = jnp.where(slot_j < slot_length, (starts + slot_j - 64 * l) % 256, -1)
    rows = jnp.arange(256, dtype=jnp.int32)
    select = rank[None, :] == rows[:, None]
    hidden = dot(select.astype(jnp.float32), slots[:, :wide])
    labels = jnp.sum(jnp.where(select, slot_target[None, :], 0), axis=1)
    owned = (slot_owner[None, :] == source[:, None]) & (slot_j[None, :] == slot_j[:, None])
    sent_rank = jnp.sum(jnp.where(owned, rank[None, :] + 1, 0), axis=1) - 1
    deliver = (sent_rank[:, None] == rows[None, :]).astype(jnp.float32)

    head = jnp.zeros((4, depth, quarter), jnp.float32)
    for s, piece in enumerate(pieces):
        head = lax.dynamic_update_slice(head, piece[None], ((x - s) % 4, 0, 0))
    head = lax.optimization_barrier(head.reshape(wide, quarter))

    partial = dot(hidden, head)
    block = partial[:64] + shift_z(partial[64:128], 1) + shift_z(partial[192:], -1) + shift_far(partial[128:192])
    logits = jnp.sum(swap(block.reshape(4, 16, quarter), "h"), axis=0)

    row_labels = lax.dynamic_slice(labels, (h * 16,), (16,))
    column = jnp.arange(quarter, dtype=jnp.int32) + j * columns + x * quarter
    onehot = (column[None, :] == row_labels[:, None]).astype(jnp.float32)
    peak = jnp.max(logits, axis=1)
    shifted = jnp.exp(logits - peak[:, None])
    stats = jnp.stack([peak, jnp.sum(shifted, axis=1), jnp.sum(logits * onehot, axis=1)], axis=0)
    stats = spread(stats, XYC, 32)
    row_peak = jnp.max(stats[:, 0], axis=0)
    exp_total = jnp.sum(stats[:, 1] * jnp.exp(stats[:, 0] - row_peak[None]), axis=0)
    logprobs = jnp.sum(stats[:, 2], axis=0) - row_peak - jnp.log(exp_total)
    scale = jnp.exp(peak - row_peak) / exp_total
    grad = onehot - shifted * scale[:, None]

    own = spread(grad, "h", 4).reshape(64, quarter)
    grads = jnp.concatenate([own, shift_z(own, -1), shift_far(own), shift_z(own, 1)], axis=0)

    grad_rows = dot(grads, head, (1, 1), GRAD)
    leaving = dot(deliver, grad_rows, (1, 0), GRAD).reshape(32, 16, wide)
    summed = jnp.sum(swap(leaving, XYC), axis=0)

    grad_head = dot(hidden, grads, (0, 0), GRAD).reshape(4, depth, quarter)
    summed, grad_head_later = lax.optimization_barrier((summed, grad_head))
    grad_weight = jnp.zeros((depth, columns), jnp.float32)
    for s in (0, 1, 3, 2):
        part = lax.dynamic_index_in_dim(grad_head_later if s == 2 else grad_head, (x + s) % 4, 0, False)
        part = shift_x(part, s) if s else part
        grad_weight = lax.dynamic_update_slice(grad_weight, part, (0, (x - s) % 4 * quarter))

    parts = lax.dynamic_update_slice(jnp.zeros((16, META), jnp.float32), logprobs.reshape(4, 4), (h * 4, 0))
    parts = jnp.where(l == x, parts, 0.0)
    arrived = swap(jnp.concatenate([summed, parts], axis=1).reshape(16, 1, wide + META), Z)[:, 0]
    slot = arrived[:, :wide].reshape(16, 4, depth).transpose(1, 0, 2).reshape(width)
    grad_hidden = spread(slot, YC, 8)
    return jnp.sum(arrived[:, wide : wide + 4], axis=0), grad_hidden, grad_weight


def solution(mesh):
    grid = Mesh(mesh.devices.reshape(4, 4, 4, 4, 2), ("x", "h", "l", "y", "c"))
    dp = ("x", "h", "l")
    placed = (P(dp, None), P(dp, YC), P(dp), P(dp), P(dp))
    return jax.shard_map(
        on_device,
        mesh=grid,
        in_specs=placed,
        out_specs=(P(dp), P(dp, None), P(dp, YC)),
        check_vma=False,
    )
```

```python
import jax
import jax.numpy as jnp
from jax import lax
from jax.sharding import Mesh, PartitionSpec as P

HIGH = lax.Precision.HIGHEST
GRAD = lax.Precision.HIGH
Z = ("h", "l")
XYC = ("x", "y", "c")
YC = ("y", "c")
META = 128


def swap(blocks, axes):
    return lax.all_to_all(blocks, axes, split_axis=0, concat_axis=0, tiled=True)


def spread(block, axes, count):
    return swap(jnp.broadcast_to(block[None], (count, *block.shape)), axes)


def shift_z(block, step):
    return lax.ppermute(block, Z, [(i, (i + step) % 16) for i in range(16)])


def shift_far(block, sign):
    step = [2 * sign, -2 * sign]
    pairs = [(2 * i + c, 2 * ((i + step[c]) % 16) + c) for i in range(16) for c in range(2)]
    return lax.ppermute(block, ("h", "l", "c"), pairs)


def shift_x(block, step):
    return lax.ppermute(block, "x", [(i, (i + step) % 4) for i in range(4)])


def dot(a, b, contract=(1, 0), precision=HIGH):
    dims = (((contract[0],), (contract[1],)), ((), ()))
    return lax.dot_general(a, b, dims, precision=precision, preferred_element_type=jnp.float32)


def on_device(responses, weight, lengths, targets, owners):
    width = responses.shape[1]
    depth, columns = weight.shape
    quarter = columns // 4
    wide = 4 * depth
    x, h, l = lax.axis_index("x"), lax.axis_index("h"), lax.axis_index("l")
    j, c = lax.axis_index(YC), lax.axis_index("c")

    def cut(array, s):
        return lax.dynamic_slice(array, (0, (x + s) % 4 * quarter), (depth, quarter))

    row = lax.dynamic_slice(responses, (j, 0), (1, width)).reshape(4, 16, depth)
    notes = jnp.pad(jnp.concatenate([targets, lengths, owners]).astype(jnp.float32), (0, META - 10))
    notes = jnp.broadcast_to(notes, (16, META))
    packed = jnp.concatenate([row.transpose(1, 0, 2).reshape(16, wide), notes], axis=1)
    packed, weight_later = lax.optimization_barrier((packed, weight))
    first = shift_x(cut(weight, 1), 1)
    pieces = [cut(weight_later, 0), first, shift_x(cut(weight_later, 2), 2), shift_x(cut(weight_later, 3), 3)]
    mine = swap(packed.reshape(16, 1, wide + META), Z).reshape(16, wide + META)
    mine, pieces[1] = lax.optimization_barrier((mine, pieces[1]))
    slots = spread(mine, XYC, 32).reshape(512, wide + META)

    ids = jnp.arange(512, dtype=jnp.int32)
    slot_j = (ids // 16) % 8
    source = (ids // 128) * 16 + ids % 16
    notes_all = slots[:, wide : wide + 10].astype(jnp.int32)
    slot_length, slot_owner = notes_all[:, 8], notes_all[:, 9]
    slot_target = jnp.sum(jnp.where(jnp.arange(10)[None, :] == slot_j[:, None], notes_all, 0), axis=1)
    before = (source[None, :] < source[:, None]) & (slot_j[None, :] == 0)
    starts = jnp.sum(jnp.where(before, slot_length[None, :], 0), axis=1)
    rank = starts + slot_j
    turn = (rank // 64 - l) % 4
    partner = h * 4 + l + jnp.where(turn == 3, -1, jnp.where((turn == 2) & (c == 1), -2, turn))
    group = (rank // 16 - partner % 16 // 4) % 4
    rank = jnp.where(slot_j < slot_length, turn * 64 + group * 16 + rank % 16, -1)
    rows = jnp.arange(256, dtype=jnp.int32)
    select = rank[None, :] == rows[:, None]
    hidden = dot(select.astype(jnp.float32), slots[:, :wide])
    labels = jnp.sum(jnp.where(select, slot_target[None, :], 0), axis=1)
    owned = (slot_owner[None, :] == source[:, None]) & (slot_j[None, :] == slot_j[:, None])
    sent_rank = jnp.sum(jnp.where(owned, rank[None, :] + 1, 0), axis=1) - 1
    deliver = (sent_rank[:, None] == rows[None, :]).astype(jnp.float32)

    head = jnp.zeros((4, depth, quarter), jnp.float32)
    for s, piece in enumerate(pieces):
        head = lax.dynamic_update_slice(head, piece[None], ((x - s) % 4, 0, 0))
    head = lax.optimization_barrier(head.reshape(wide, quarter))

    partial = dot(hidden, head)
    block = partial[:64] + shift_z(partial[64:128], 1) + shift_z(partial[192:], -1) + shift_far(partial[128:192], 1)
    logits = block[:16] + shift_z(block[16:32], 4) + shift_z(block[32:48], 8) + shift_z(block[48:], -4)

    row_labels = labels[:16]
    column = jnp.arange(quarter, dtype=jnp.int32) + j * columns + x * quarter
    onehot = (column[None, :] == row_labels[:, None]).astype(jnp.float32)
    peak = jnp.max(logits, axis=1)
    shifted = jnp.exp(logits - peak[:, None])
    stats = jnp.stack([peak, jnp.sum(shifted, axis=1), jnp.sum(logits * onehot, axis=1)], axis=0)
    stats = spread(stats, XYC, 32)
    row_peak = jnp.max(stats[:, 0], axis=0)
    exp_total = jnp.sum(stats[:, 1] * jnp.exp(stats[:, 0] - row_peak[None]), axis=0)
    logprobs = jnp.sum(stats[:, 2], axis=0) - row_peak - jnp.log(exp_total)
    scale = jnp.exp(peak - row_peak) / exp_total
    grad = onehot - shifted * scale[:, None]

    own = jnp.concatenate([grad, shift_z(grad, -4), shift_z(grad, 8), shift_z(grad, 4)], axis=0)
    grads = jnp.concatenate([own, shift_z(own, -1), shift_far(own, -1), shift_z(own, 1)], axis=0)

    grad_rows = dot(grads, head, (1, 1), GRAD)
    leaving = dot(deliver, grad_rows, (1, 0), GRAD).reshape(32, 16, wide)
    summed = jnp.sum(swap(leaving, XYC), axis=0)

    grad_head = dot(hidden, grads, (0, 0), GRAD).reshape(4, depth, quarter)
    summed, grad_head_later = lax.optimization_barrier((summed, grad_head))
    grad_weight = jnp.zeros((depth, columns), jnp.float32)
    for s in (0, 1, 3, 2):
        part = lax.dynamic_index_in_dim(grad_head_later if s == 2 else grad_head, (x + s) % 4, 0, False)
        part = shift_x(part, s) if s else part
        grad_weight = lax.dynamic_update_slice(grad_weight, part, (0, (x - s) % 4 * quarter))

    parts = lax.dynamic_update_slice(jnp.zeros((16, META), jnp.float32), logprobs.reshape(4, 4), (h * 4, 0))
    parts = jnp.where(l == x, parts, 0.0)
    arrived = swap(jnp.concatenate([summed, parts], axis=1).reshape(16, 1, wide + META), Z)[:, 0]
    slot = arrived[:, :wide].reshape(16, 4, depth).transpose(1, 0, 2).reshape(width)
    grad_hidden = spread(slot, YC, 8)
    return jnp.sum(arrived[:, wide : wide + 4], axis=0), grad_hidden, grad_weight


def solution(mesh):
    grid = Mesh(mesh.devices.reshape(4, 4, 4, 4, 2), ("x", "h", "l", "y", "c"))
    dp = ("x", "h", "l")
    placed = (P(dp, None), P(dp, YC), P(dp), P(dp), P(dp))
    return jax.shard_map(
        on_device,
        mesh=grid,
        in_specs=placed,
        out_specs=(P(dp), P(dp, None), P(dp, YC)),
        check_vma=False,
    )
```

```python
import jax
import jax.numpy as jnp
from jax import lax
from jax.sharding import Mesh, PartitionSpec as P

HIGH = lax.Precision.HIGHEST
GRAD = lax.Precision.HIGH
Z = ("h", "l")
XYC = ("x", "y", "c")
YC = ("y", "c")
META = 128


def swap(blocks, axes):
    return lax.all_to_all(blocks, axes, split_axis=0, concat_axis=0, tiled=True)


def spread(block, axes, count):
    return swap(jnp.broadcast_to(block[None], (count, *block.shape)), axes)


def shift_z(block, step):
    return lax.ppermute(block, Z, [(i, (i + step) % 16) for i in range(16)])


def shift_far(block):
    pairs = [(2 * i + c, 2 * ((i + 2 - 4 * c) % 16) + c) for i in range(16) for c in range(2)]
    return lax.ppermute(block, ("h", "l", "c"), pairs)


def shift_x(block, step):
    return lax.ppermute(block, "x", [(i, (i + step) % 4) for i in range(4)])


def dot(a, b, contract=(1, 0), precision=HIGH):
    dims = (((contract[0],), (contract[1],)), ((), ()))
    return lax.dot_general(a, b, dims, precision=precision, preferred_element_type=jnp.float32)


def on_device(responses, weight, lengths, targets, owners):
    width = responses.shape[1]
    depth, columns = weight.shape
    quarter = columns // 4
    wide = 4 * depth
    x, h, l = lax.axis_index("x"), lax.axis_index("h"), lax.axis_index("l")
    j, c = lax.axis_index(YC), lax.axis_index("c")

    row = lax.dynamic_slice(responses, (j, 0), (1, width)).reshape(4, 16, depth)
    notes = jnp.pad(jnp.concatenate([targets, lengths, owners]).astype(jnp.float32), (0, META - 10))
    notes = jnp.broadcast_to(notes, (16, META))
    packed = jnp.concatenate([row.transpose(1, 0, 2).reshape(16, wide), notes], axis=1)
    def cut(array, s):
        return lax.dynamic_slice(array, (0, (x + s) % 4 * quarter), (depth, quarter))

    packed, weight = lax.optimization_barrier((packed, weight))
    pieces = [cut(weight, 0), shift_x(cut(weight, 1), 1), shift_x(cut(weight, 2), 2)]
    mine = swap(packed.reshape(16, 1, wide + META), Z).reshape(16, wide + META)
    mine, weight = lax.optimization_barrier((mine, weight))
    pieces.append(shift_x(cut(weight, 3), 3))

    slots = spread(mine, ("x", "y"), 16).reshape(256, wide + META)
    slots, pieces[2], pieces[3] = lax.optimization_barrier((slots, pieces[2], pieces[3]))
    slots_other = lax.ppermute(slots, "c", [(0, 1), (1, 0)])

    all_notes = slots[:, wide : wide + 10].astype(jnp.int32)
    source_notes = all_notes.reshape(4, 4, 16, 10)[:, 0].reshape(64, 10)
    source_length, source_owner = source_notes[:, 8], source_notes[:, 9]
    sources = jnp.arange(64, dtype=jnp.int32)

    def starts_of(source):
        return jnp.sum(jnp.where(sources[None, :] < source[:, None], source_length[None, :], 0), axis=1)

    rows = jnp.arange(256, dtype=jnp.int32)
    starts = starts_of(rows // 64 * 16 + rows % 16)

    def chosen(core):
        slot_j = rows // 16 % 4 * 2 + core
        rank = jnp.where(slot_j < all_notes[:, 8], (starts + slot_j - 64 * l) % 256, -1)
        target = jnp.sum(jnp.where(jnp.arange(10)[None, :] == slot_j[:, None], all_notes, 0), axis=1)
        select = rank[None, :] == rows[:, None]
        return select.astype(jnp.float32), jnp.sum(jnp.where(select, target[None, :], 0), axis=1)

    select, labels = chosen(c)
    select_other, labels_other = chosen(1 - c)
    labels = labels + labels_other
    hidden = dot(select, slots[:, :wide]) + dot(select_other, slots_other[:, :wide])

    ids = jnp.arange(512, dtype=jnp.int32)
    slot_j = ids // 16 % 8
    owned = source_owner[None, :] == (ids // 128 * 16 + ids % 16)[:, None]
    sent_start = jnp.sum(jnp.where(owned, starts_of(sources)[None, :], 0), axis=1)
    sent_length = jnp.sum(jnp.where(owned, source_length[None, :], 0), axis=1)
    sent_rank = jnp.where(slot_j < sent_length, (sent_start + slot_j - 64 * l) % 256, -1)
    deliver = (sent_rank[:, None] == rows[None, :]).astype(jnp.float32)

    head = jnp.zeros((4, depth, quarter), jnp.float32)
    for s, piece in enumerate(pieces):
        head = lax.dynamic_update_slice(head, piece[None], ((x - s) % 4, 0, 0))
    head = lax.optimization_barrier(head.reshape(wide, quarter))

    partial = dot(hidden, head)
    block = partial[:64] + shift_z(partial[64:128], 1) + shift_z(partial[192:], -1) + shift_far(partial[128:192])
    logits = jnp.sum(swap(block.reshape(4, 16, quarter), "h"), axis=0)

    row_labels = lax.dynamic_slice(labels, (h * 16,), (16,))
    column = jnp.arange(quarter, dtype=jnp.int32) + j * columns + x * quarter
    onehot = (column[None, :] == row_labels[:, None]).astype(jnp.float32)
    peak = jnp.max(logits, axis=1)
    shifted = jnp.exp(logits - peak[:, None])
    stats = jnp.stack([peak, jnp.sum(shifted, axis=1), jnp.sum(logits * onehot, axis=1)], axis=0)
    stats = spread(stats, XYC, 32)
    row_peak = jnp.max(stats[:, 0], axis=0)
    exp_total = jnp.sum(stats[:, 1] * jnp.exp(stats[:, 0] - row_peak[None]), axis=0)
    logprobs = jnp.sum(stats[:, 2], axis=0) - row_peak - jnp.log(exp_total)
    scale = jnp.exp(peak - row_peak) / exp_total
    grad = onehot - shifted * scale[:, None]

    own = spread(grad, "h", 4).reshape(64, quarter)
    grads = jnp.concatenate([own, shift_z(own, -1), shift_far(own), shift_z(own, 1)], axis=0)

    grad_rows = dot(grads, head, (1, 1), GRAD)
    leaving = dot(deliver, grad_rows, (1, 0), GRAD).reshape(32, 16, wide)
    summed = jnp.sum(swap(leaving, XYC), axis=0)

    grad_head = dot(hidden, grads, (0, 0), GRAD).reshape(4, depth, quarter)
    grad_weight = jnp.zeros((depth, columns), jnp.float32)
    for s in (0, 1, 3, 2):
        part = lax.dynamic_index_in_dim(grad_head, (x + s) % 4, 0, False)
        part = shift_x(part, s) if s else part
        grad_weight = lax.dynamic_update_slice(grad_weight, part, (0, (x - s) % 4 * quarter))

    parts = lax.dynamic_update_slice(jnp.zeros((16, META), jnp.float32), logprobs.reshape(4, 4), (h * 4, 0))
    parts = jnp.where(l == x, parts, 0.0)
    arrived = swap(jnp.concatenate([summed, parts], axis=1).reshape(16, 1, wide + META), Z)[:, 0]
    slot = arrived[:, :wide].reshape(16, 4, depth).transpose(1, 0, 2).reshape(width)
    grad_hidden = spread(slot, YC, 8)
    return jnp.sum(arrived[:, wide : wide + 4], axis=0), grad_hidden, grad_weight


def solution(mesh):
    grid = Mesh(mesh.devices.reshape(4, 4, 4, 4, 2), ("x", "h", "l", "y", "c"))
    dp = ("x", "h", "l")
    placed = (P(dp, None), P(dp, YC), P(dp), P(dp), P(dp))
    return jax.shard_map(
        on_device,
        mesh=grid,
        in_specs=placed,
        out_specs=(P(dp), P(dp, None), P(dp, YC)),
        check_vma=False,
    )
```

```python
import jax
import jax.numpy as jnp
from jax import lax
from jax.sharding import Mesh, PartitionSpec as P

HIGH = lax.Precision.HIGHEST
GRAD = lax.Precision.HIGH
Z = ("h", "l")
XYC = ("x", "y", "c")
YC = ("y", "c")
META = 128


def swap(blocks, axes):
    return lax.all_to_all(blocks, axes, split_axis=0, concat_axis=0, tiled=True)


def spread(block, axes, count):
    return swap(jnp.broadcast_to(block[None], (count, *block.shape)), axes)


def shift_z(block, step):
    return lax.ppermute(block, Z, [(i, (i + step) % 16) for i in range(16)])


def shift_far(block):
    pairs = [(2 * i + c, 2 * ((i + 2 - 4 * c) % 16) + c) for i in range(16) for c in range(2)]
    return lax.ppermute(block, ("h", "l", "c"), pairs)


def shift_x(block, step):
    return lax.ppermute(block, "x", [(i, (i + step) % 4) for i in range(4)])


def dot(a, b, contract=(1, 0), precision=HIGH):
    dims = (((contract[0],), (contract[1],)), ((), ()))
    return lax.dot_general(a, b, dims, precision=precision, preferred_element_type=jnp.float32)


def on_device(responses, weight, lengths, targets, owners):
    width = responses.shape[1]
    depth, columns = weight.shape
    quarter = columns // 4
    wide = 4 * depth
    x, h, l = lax.axis_index("x"), lax.axis_index("h"), lax.axis_index("l")
    j = lax.axis_index(YC)

    row = lax.dynamic_slice(responses, (j, 0), (1, width)).reshape(4, 16, depth)
    notes = jnp.pad(jnp.concatenate([targets, lengths, owners]).astype(jnp.float32), (0, META - 10))
    notes = jnp.broadcast_to(notes, (16, META))
    packed = jnp.concatenate([row.transpose(1, 0, 2).reshape(16, wide), notes], axis=1)
    def cut(array, s):
        return lax.dynamic_slice(array, (0, (x + s) % 4 * quarter), (depth, quarter))

    packed, weight = lax.optimization_barrier((packed, weight))
    pieces = [cut(weight, 0), shift_x(cut(weight, 1), 1), shift_x(cut(weight, 2), 2)]
    mine = swap(packed.reshape(16, 1, wide + META), Z).reshape(16, wide + META)
    mine, weight = lax.optimization_barrier((mine, weight))
    pieces.append(shift_x(cut(weight, 3), 3))
    slots = spread(mine, XYC, 32).reshape(512, wide + META)
    ids = jnp.arange(512, dtype=jnp.int32)
    slot_j = (ids // 16) % 8
    source = (ids // 128) * 16 + ids % 16
    notes_all = slots[:, wide : wide + 10].astype(jnp.int32)
    slot_length, slot_owner = notes_all[:, 8], notes_all[:, 9]
    slot_target = jnp.sum(jnp.where(jnp.arange(10)[None, :] == slot_j[:, None], notes_all, 0), axis=1)
    before = (source[None, :] < source[:, None]) & (slot_j[None, :] == 0)
    starts = jnp.sum(jnp.where(before, slot_length[None, :], 0), axis=1)
    rank = jnp.where(slot_j < slot_length, (starts + slot_j - 64 * l) % 256, -1)
    rows = jnp.arange(256, dtype=jnp.int32)
    select = rank[None, :] == rows[:, None]
    hidden = dot(select.astype(jnp.float32), slots[:, :wide])
    labels = jnp.sum(jnp.where(select, slot_target[None, :], 0), axis=1)
    owned = (slot_owner[None, :] == source[:, None]) & (slot_j[None, :] == slot_j[:, None])
    sent_rank = jnp.sum(jnp.where(owned, rank[None, :] + 1, 0), axis=1) - 1
    deliver = (sent_rank[:, None] == rows[None, :]).astype(jnp.float32)

    head = jnp.zeros((4, depth, quarter), jnp.float32)
    for s, piece in enumerate(pieces):
        head = lax.dynamic_update_slice(head, piece[None], ((x - s) % 4, 0, 0))
    head = lax.optimization_barrier(head.reshape(wide, quarter))

    partial = dot(hidden, head)
    block = partial[:64] + shift_z(partial[64:128], 1) + shift_z(partial[192:], -1) + shift_far(partial[128:192])
    logits = jnp.sum(swap(block.reshape(4, 16, quarter), "h"), axis=0)

    row_labels = lax.dynamic_slice(labels, (h * 16,), (16,))
    column = jnp.arange(quarter, dtype=jnp.int32) + j * columns + x * quarter
    onehot = (column[None, :] == row_labels[:, None]).astype(jnp.float32)
    peak = jnp.max(logits, axis=1)
    shifted = jnp.exp(logits - peak[:, None])
    stats = jnp.stack([peak, jnp.sum(shifted, axis=1), jnp.sum(logits * onehot, axis=1)], axis=0)
    stats = spread(stats, XYC, 32)
    row_peak = jnp.max(stats[:, 0], axis=0)
    exp_total = jnp.sum(stats[:, 1] * jnp.exp(stats[:, 0] - row_peak[None]), axis=0)
    logprobs = jnp.sum(stats[:, 2], axis=0) - row_peak - jnp.log(exp_total)
    scale = jnp.exp(peak - row_peak) / exp_total
    grad = onehot - shifted * scale[:, None]

    own = spread(grad, "h", 4).reshape(64, quarter)
    grads = jnp.concatenate([own, shift_z(own, -1), shift_far(own), shift_z(own, 1)], axis=0)

    grad_rows = dot(grads, head, (1, 1), GRAD)
    leaving = dot(deliver, grad_rows, (1, 0), GRAD).reshape(32, 16, wide)
    summed = jnp.sum(swap(leaving, XYC), axis=0)

    grad_head = dot(hidden, grads, (0, 0), GRAD).reshape(4, depth, quarter)
    summed, grad_head_later = lax.optimization_barrier((summed, grad_head))

    def part(array, s):
        return lax.dynamic_index_in_dim(array, (x + s) % 4, 0, False)

    grad_weight = jnp.tile(part(grad_head_later, 0), (1, 4))
    for s in (1, 3, 2):
        grad_weight = lax.dynamic_update_slice(grad_weight, shift_x(part(grad_head, s), s), (0, (x - s) % 4 * quarter))

    parts = lax.dynamic_update_slice(jnp.zeros((16, META), jnp.float32), logprobs.reshape(4, 4), (h * 4, 0))
    parts = jnp.where(l == x, parts, 0.0)
    arrived = swap(jnp.concatenate([summed, parts], axis=1).reshape(16, 1, wide + META), Z)[:, 0]
    slot = arrived[:, :wide].reshape(16, 4, depth).transpose(1, 0, 2).reshape(width)
    grad_hidden = spread(slot, YC, 8)
    return jnp.sum(arrived[:, wide : wide + 4], axis=0), grad_hidden, grad_weight


def solution(mesh):
    grid = Mesh(mesh.devices.reshape(4, 4, 4, 4, 2), ("x", "h", "l", "y", "c"))
    dp = ("x", "h", "l")
    placed = (P(dp, None), P(dp, YC), P(dp), P(dp), P(dp))
    return jax.shard_map(
        on_device,
        mesh=grid,
        in_specs=placed,
        out_specs=(P(dp), P(dp, None), P(dp, YC)),
        check_vma=False,
    )
```

```python
import jax
import jax.numpy as jnp
from jax import lax
from jax.sharding import Mesh, PartitionSpec as P

HIGH = lax.Precision.HIGHEST
GRAD = lax.Precision.HIGH
Z = ("h", "l")
XYC = ("x", "y", "c")
YC = ("y", "c")
META = 128


def swap(blocks, axes):
    return lax.all_to_all(blocks, axes, split_axis=0, concat_axis=0, tiled=True)


def spread(block, axes, count):
    return swap(jnp.broadcast_to(block[None], (count, *block.shape)), axes)


def shift_z(block, step):
    return lax.ppermute(block, Z, [(i, (i + step) % 16) for i in range(16)])


def shift_far(block):
    pairs = [(2 * i + c, 2 * ((i + 2 - 4 * c) % 16) + c) for i in range(16) for c in range(2)]
    return lax.ppermute(block, ("h", "l", "c"), pairs)


def shift_x(block, step):
    return lax.ppermute(block, "x", [(i, (i + step) % 4) for i in range(4)])


def dot(a, b, contract=(1, 0), precision=HIGH):
    dims = (((contract[0],), (contract[1],)), ((), ()))
    return lax.dot_general(a, b, dims, precision=precision, preferred_element_type=jnp.float32)


def on_device(responses, weight, lengths, targets, owners):
    width = responses.shape[1]
    depth, columns = weight.shape
    quarter = columns // 4
    wide = 4 * depth
    x, h, l = lax.axis_index("x"), lax.axis_index("h"), lax.axis_index("l")
    j, c = lax.axis_index(YC), lax.axis_index("c")

    row = lax.dynamic_slice(responses, (j, 0), (1, width)).reshape(4, 16, depth)
    notes = jnp.pad(jnp.concatenate([targets, lengths, owners]).astype(jnp.float32), (0, META - 10))
    notes = jnp.broadcast_to(notes, (16, META))
    packed = jnp.concatenate([row.transpose(1, 0, 2).reshape(16, wide), notes], axis=1)
    def cut(array, s):
        return lax.dynamic_slice(array, (0, (x + s) % 4 * quarter), (depth, quarter))

    first = shift_x(cut(weight, 1), 1)
    packed, weight = lax.optimization_barrier((packed, weight))
    pieces = [cut(weight, 0), first, shift_x(cut(weight, 2), 2), shift_x(cut(weight, 3), 3)]
    mine = swap(packed.reshape(16, 1, wide + META), Z).reshape(16, wide + META)

    slots = spread(mine, ("x", "y"), 16).reshape(256, wide + META)
    slots, pieces[3] = lax.optimization_barrier((slots, pieces[3]))
    slots_other = lax.ppermute(slots, "c", [(0, 1), (1, 0)])

    all_notes = slots[:, wide : wide + 10].astype(jnp.int32)
    source_notes = all_notes.reshape(4, 4, 16, 10)[:, 0].reshape(64, 10)
    source_length, source_owner = source_notes[:, 8], source_notes[:, 9]
    sources = jnp.arange(64, dtype=jnp.int32)

    def starts_of(source):
        return jnp.sum(jnp.where(sources[None, :] < source[:, None], source_length[None, :], 0), axis=1)

    rows = jnp.arange(256, dtype=jnp.int32)
    starts = starts_of(rows // 64 * 16 + rows % 16)

    def chosen(core):
        slot_j = rows // 16 % 4 * 2 + core
        rank = jnp.where(slot_j < all_notes[:, 8], (starts + slot_j - 64 * l) % 256, -1)
        target = jnp.sum(jnp.where(jnp.arange(10)[None, :] == slot_j[:, None], all_notes, 0), axis=1)
        select = rank[None, :] == rows[:, None]
        return select.astype(jnp.float32), jnp.sum(jnp.where(select, target[None, :], 0), axis=1)

    select, labels = chosen(c)
    select_other, labels_other = chosen(1 - c)
    labels = labels + labels_other
    hidden = dot(select, slots[:, :wide]) + dot(select_other, slots_other[:, :wide])

    ids = jnp.arange(512, dtype=jnp.int32)
    slot_j = ids // 16 % 8
    owned = source_owner[None, :] == (ids // 128 * 16 + ids % 16)[:, None]
    sent_start = jnp.sum(jnp.where(owned, starts_of(sources)[None, :], 0), axis=1)
    sent_length = jnp.sum(jnp.where(owned, source_length[None, :], 0), axis=1)
    sent_rank = jnp.where(slot_j < sent_length, (sent_start + slot_j - 64 * l) % 256, -1)
    deliver = (sent_rank[:, None] == rows[None, :]).astype(jnp.float32)

    head = jnp.zeros((4, depth, quarter), jnp.float32)
    for s, piece in enumerate(pieces):
        head = lax.dynamic_update_slice(head, piece[None], ((x - s) % 4, 0, 0))
    head = lax.optimization_barrier(head.reshape(wide, quarter))

    partial = dot(hidden, head)
    block = partial[:64] + shift_z(partial[64:128], 1) + shift_z(partial[192:], -1) + shift_far(partial[128:192])
    logits = jnp.sum(swap(block.reshape(4, 16, quarter), "h"), axis=0)

    row_labels = lax.dynamic_slice(labels, (h * 16,), (16,))
    column = jnp.arange(quarter, dtype=jnp.int32) + j * columns + x * quarter
    onehot = (column[None, :] == row_labels[:, None]).astype(jnp.float32)
    peak = jnp.max(logits, axis=1)
    shifted = jnp.exp(logits - peak[:, None])
    stats = jnp.stack([peak, jnp.sum(shifted, axis=1), jnp.sum(logits * onehot, axis=1)], axis=0)
    stats = spread(stats, XYC, 32)
    row_peak = jnp.max(stats[:, 0], axis=0)
    exp_total = jnp.sum(stats[:, 1] * jnp.exp(stats[:, 0] - row_peak[None]), axis=0)
    logprobs = jnp.sum(stats[:, 2], axis=0) - row_peak - jnp.log(exp_total)
    scale = jnp.exp(peak - row_peak) / exp_total
    grad = onehot - shifted * scale[:, None]

    own = spread(grad, "h", 4).reshape(64, quarter)
    grads = jnp.concatenate([own, shift_z(own, -1), shift_far(own), shift_z(own, 1)], axis=0)

    grad_rows = dot(grads, head, (1, 1), GRAD)
    leaving = dot(deliver, grad_rows, (1, 0), GRAD).reshape(32, 16, wide)
    summed = jnp.sum(swap(leaving, XYC), axis=0)

    grad_head = dot(hidden, grads, (0, 0), GRAD).reshape(4, depth, quarter)
    summed, grad_head_later = lax.optimization_barrier((summed, grad_head))

    def part(array, s):
        return lax.dynamic_index_in_dim(array, (x + s) % 4, 0, False)

    grad_weight = jnp.tile(part(grad_head_later, 0), (1, 4))
    for s in (1, 3, 2):
        grad_weight = lax.dynamic_update_slice(grad_weight, shift_x(part(grad_head, s), s), (0, (x - s) % 4 * quarter))

    parts = lax.dynamic_update_slice(jnp.zeros((16, META), jnp.float32), logprobs.reshape(4, 4), (h * 4, 0))
    parts = jnp.where(l == x, parts, 0.0)
    arrived = swap(jnp.concatenate([summed, parts], axis=1).reshape(16, 1, wide + META), Z)[:, 0]
    slot = arrived[:, :wide].reshape(16, 4, depth).transpose(1, 0, 2).reshape(width)
    grad_hidden = spread(slot, YC, 8)
    return jnp.sum(arrived[:, wide : wide + 4], axis=0), grad_hidden, grad_weight


def solution(mesh):
    grid = Mesh(mesh.devices.reshape(4, 4, 4, 4, 2), ("x", "h", "l", "y", "c"))
    dp = ("x", "h", "l")
    placed = (P(dp, None), P(dp, YC), P(dp), P(dp), P(dp))
    return jax.shard_map(
        on_device,
        mesh=grid,
        in_specs=placed,
        out_specs=(P(dp), P(dp, None), P(dp, YC)),
        check_vma=False,
    )
```

```python
import jax
import jax.numpy as jnp
from jax import lax
from jax.sharding import Mesh, PartitionSpec as P

HIGH = lax.Precision.HIGHEST
GRAD = lax.Precision.HIGH
Z = ("h", "l")
XYC = ("x", "y", "c")
YC = ("y", "c")
META = 128


def swap(blocks, axes):
    return lax.all_to_all(blocks, axes, split_axis=0, concat_axis=0, tiled=True)


def spread(block, axes, count):
    return swap(jnp.broadcast_to(block[None], (count, *block.shape)), axes)


def shift_z(block, step):
    return lax.ppermute(block, Z, [(i, (i + step) % 16) for i in range(16)])


def shift_far(block):
    pairs = [(2 * i + c, 2 * ((i + 2 - 4 * c) % 16) + c) for i in range(16) for c in range(2)]
    return lax.ppermute(block, ("h", "l", "c"), pairs)


def shift_x(block, step):
    return lax.ppermute(block, "x", [(i, (i + step) % 4) for i in range(4)])


def dot(a, b, contract=(1, 0), precision=HIGH):
    dims = (((contract[0],), (contract[1],)), ((), ()))
    return lax.dot_general(a, b, dims, precision=precision, preferred_element_type=jnp.float32)


def on_device(responses, weight, lengths, targets, owners):
    width = responses.shape[1]
    depth, columns = weight.shape
    quarter = columns // 4
    wide = 4 * depth
    x, h, l = lax.axis_index("x"), lax.axis_index("h"), lax.axis_index("l")
    j, c = lax.axis_index(YC), lax.axis_index("c")

    row = lax.dynamic_slice(responses, (j, 0), (1, width)).reshape(4, 16, depth)
    notes = jnp.pad(jnp.concatenate([targets, lengths, owners]).astype(jnp.float32), (0, META - 10))
    notes = jnp.broadcast_to(notes, (16, META))
    packed = jnp.concatenate([row.transpose(1, 0, 2).reshape(16, wide), notes], axis=1).reshape(1, 16, 1, wide + META)
    packed = jnp.broadcast_to(packed, (4, 16, 1, wide + META)).reshape(64, 1, wide + META)

    def cut(array, s):
        return lax.dynamic_slice(array, (0, (x + s) % 4 * quarter), (depth, quarter))

    packed, weight = lax.optimization_barrier((packed, weight))
    pieces = [cut(weight, 0), *(shift_x(cut(weight, s), s) for s in range(1, 4))]
    mine = swap(packed, ("x", *Z)).reshape(64, wide + META)

    slots = spread(mine, "y", 4).reshape(256, wide + META)
    slots, pieces[3] = lax.optimization_barrier((slots, pieces[3]))
    slots_other = lax.ppermute(slots, "c", [(0, 1), (1, 0)])

    all_notes = slots[:, wide : wide + 10].astype(jnp.int32)
    source_length, source_owner = all_notes[:64, 8], all_notes[:64, 9]
    sources = jnp.arange(64, dtype=jnp.int32)

    def starts_of(source):
        return jnp.sum(jnp.where(sources[None, :] < source[:, None], source_length[None, :], 0), axis=1)

    rows = jnp.arange(256, dtype=jnp.int32)
    starts = starts_of(rows % 64)

    def chosen(core):
        slot_j = rows // 64 * 2 + core
        rank = jnp.where(slot_j < all_notes[:, 8], (starts + slot_j - 64 * l) % 256, -1)
        target = jnp.sum(jnp.where(jnp.arange(10)[None, :] == slot_j[:, None], all_notes, 0), axis=1)
        select = rank[None, :] == rows[:, None]
        return select.astype(jnp.float32), jnp.sum(jnp.where(select, target[None, :], 0), axis=1)

    select, labels = chosen(c)
    select_other, labels_other = chosen(1 - c)
    labels = labels + labels_other
    hidden = dot(select, slots[:, :wide]) + dot(select_other, slots_other[:, :wide])

    ids = jnp.arange(512, dtype=jnp.int32)
    slot_j = ids // 16 % 8
    owned = source_owner[None, :] == (ids // 128 * 16 + ids % 16)[:, None]
    sent_start = jnp.sum(jnp.where(owned, starts_of(sources)[None, :], 0), axis=1)
    sent_length = jnp.sum(jnp.where(owned, source_length[None, :], 0), axis=1)
    sent_rank = jnp.where(slot_j < sent_length, (sent_start + slot_j - 64 * l) % 256, -1)
    deliver = (sent_rank[:, None] == rows[None, :]).astype(jnp.float32)

    head = jnp.zeros((4, depth, quarter), jnp.float32)
    for s, piece in enumerate(pieces):
        head = lax.dynamic_update_slice(head, piece[None], ((x - s) % 4, 0, 0))
    head = lax.optimization_barrier(head.reshape(wide, quarter))

    partial = dot(hidden, head)
    block = partial[:64] + shift_z(partial[64:128], 1) + shift_z(partial[192:], -1) + shift_far(partial[128:192])
    logits = jnp.sum(swap(block.reshape(4, 16, quarter), "h"), axis=0)

    row_labels = lax.dynamic_slice(labels, (h * 16,), (16,))
    column = jnp.arange(quarter, dtype=jnp.int32) + j * columns + x * quarter
    onehot = (column[None, :] == row_labels[:, None]).astype(jnp.float32)
    peak = jnp.max(logits, axis=1)
    shifted = jnp.exp(logits - peak[:, None])
    stats = jnp.stack([peak, jnp.sum(shifted, axis=1), jnp.sum(logits * onehot, axis=1)], axis=0)
    stats = spread(stats, XYC, 32)
    row_peak = jnp.max(stats[:, 0], axis=0)
    exp_total = jnp.sum(stats[:, 1] * jnp.exp(stats[:, 0] - row_peak[None]), axis=0)
    logprobs = jnp.sum(stats[:, 2], axis=0) - row_peak - jnp.log(exp_total)
    scale = jnp.exp(peak - row_peak) / exp_total
    grad = onehot - shifted * scale[:, None]

    own = spread(grad, "h", 4).reshape(64, quarter)
    grads = jnp.concatenate([own, shift_z(own, -1), shift_far(own), shift_z(own, 1)], axis=0)

    grad_rows = dot(grads, head, (1, 1), GRAD)
    leaving = dot(deliver, grad_rows, (1, 0), GRAD).reshape(32, 16, wide)
    summed = jnp.sum(swap(leaving, XYC), axis=0)

    grad_head = dot(hidden, grads, (0, 0), GRAD).reshape(4, depth, quarter)
    summed, grad_head_later = lax.optimization_barrier((summed, grad_head))

    def part(array, s):
        return lax.dynamic_index_in_dim(array, (x + s) % 4, 0, False)

    grad_weight = jnp.tile(part(grad_head_later, 0), (1, 4))
    for s in (1, 3, 2):
        grad_weight = lax.dynamic_update_slice(grad_weight, shift_x(part(grad_head, s), s), (0, (x - s) % 4 * quarter))

    parts = lax.dynamic_update_slice(jnp.zeros((16, META), jnp.float32), logprobs.reshape(4, 4), (h * 4, 0))
    parts = jnp.where(l == x, parts, 0.0)
    arrived = swap(jnp.concatenate([summed, parts], axis=1).reshape(16, 1, wide + META), Z)[:, 0]
    slot = arrived[:, :wide].reshape(16, 4, depth).transpose(1, 0, 2).reshape(width)
    grad_hidden = spread(slot, YC, 8)
    return jnp.sum(arrived[:, wide : wide + 4], axis=0), grad_hidden, grad_weight


def solution(mesh):
    grid = Mesh(mesh.devices.reshape(4, 4, 4, 4, 2), ("x", "h", "l", "y", "c"))
    dp = ("x", "h", "l")
    placed = (P(dp, None), P(dp, YC), P(dp), P(dp), P(dp))
    return jax.shard_map(
        on_device,
        mesh=grid,
        in_specs=placed,
        out_specs=(P(dp), P(dp, None), P(dp, YC)),
        check_vma=False,
    )
```

```python
import jax
import jax.numpy as jnp
from jax import lax
from jax.sharding import Mesh, PartitionSpec as P

HIGH = lax.Precision.HIGHEST
GRAD = lax.Precision.HIGH
Z = ("h", "l")
XYC = ("x", "y", "c")
YC = ("y", "c")
META = 128


def swap(blocks, axes):
    return lax.all_to_all(blocks, axes, split_axis=0, concat_axis=0, tiled=True)


def spread(block, axes, count):
    return swap(jnp.broadcast_to(block[None], (count, *block.shape)), axes)


def shift_z(block, step):
    return lax.ppermute(block, Z, [(i, (i + step) % 16) for i in range(16)])


def shift_far(block):
    pairs = [(2 * i + c, 2 * ((i + 2 - 4 * c) % 16) + c) for i in range(16) for c in range(2)]
    return lax.ppermute(block, ("h", "l", "c"), pairs)


def shift_x(block, step):
    return lax.ppermute(block, "x", [(i, (i + step) % 4) for i in range(4)])


def dot(a, b, contract=(1, 0), precision=HIGH):
    dims = (((contract[0],), (contract[1],)), ((), ()))
    return lax.dot_general(a, b, dims, precision=precision, preferred_element_type=jnp.float32)


def on_device(responses, weight, lengths, targets, owners):
    width = responses.shape[1]
    depth, columns = weight.shape
    quarter = columns // 4
    wide = 4 * depth
    x, h, l = lax.axis_index("x"), lax.axis_index("h"), lax.axis_index("l")
    j, c = lax.axis_index(YC), lax.axis_index("c")

    row = lax.dynamic_slice(responses, (j, 0), (1, width)).reshape(4, 16, depth)
    notes = jnp.pad(jnp.concatenate([targets, lengths, owners]).astype(jnp.float32), (0, META - 10))
    notes = jnp.broadcast_to(notes, (16, META))
    packed = jnp.concatenate([row.transpose(1, 0, 2).reshape(16, wide), notes], axis=1).reshape(1, 16, 1, wide + META)
    packed = jnp.broadcast_to(packed, (4, 16, 1, wide + META)).reshape(64, 1, wide + META)

    def cut(array, s):
        return lax.dynamic_slice(array, (0, (x + s) % 4 * quarter), (depth, quarter))

    pieces = [cut(weight, 0), *(shift_x(cut(weight, s), s) for s in range(1, 4))]
    mine = swap(packed, ("x", *Z)).reshape(64, wide + META)
    mine, pieces[0] = lax.optimization_barrier((mine, pieces[0]))

    slots = spread(mine, "y", 4).reshape(256, wide + META)
    slots, pieces[3] = lax.optimization_barrier((slots, pieces[3]))
    slots_other = lax.ppermute(slots, "c", [(0, 1), (1, 0)])

    all_notes = slots[:, wide : wide + 10].astype(jnp.int32)
    source_length, source_owner = all_notes[:64, 8], all_notes[:64, 9]
    sources = jnp.arange(64, dtype=jnp.int32)

    def starts_of(source):
        return jnp.sum(jnp.where(sources[None, :] < source[:, None], source_length[None, :], 0), axis=1)

    rows = jnp.arange(256, dtype=jnp.int32)
    starts = starts_of(rows % 64)

    def chosen(core):
        slot_j = rows // 64 * 2 + core
        rank = jnp.where(slot_j < all_notes[:, 8], (starts + slot_j - 64 * l) % 256, -1)
        target = jnp.sum(jnp.where(jnp.arange(10)[None, :] == slot_j[:, None], all_notes, 0), axis=1)
        select = rank[None, :] == rows[:, None]
        return select.astype(jnp.float32), jnp.sum(jnp.where(select, target[None, :], 0), axis=1)

    select, labels = chosen(c)
    select_other, labels_other = chosen(1 - c)
    labels = labels + labels_other
    hidden = dot(select, slots[:, :wide]) + dot(select_other, slots_other[:, :wide])

    ids = jnp.arange(512, dtype=jnp.int32)
    slot_j = ids // 16 % 8
    owned = source_owner[None, :] == (ids // 128 * 16 + ids % 16)[:, None]
    sent_start = jnp.sum(jnp.where(owned, starts_of(sources)[None, :], 0), axis=1)
    sent_length = jnp.sum(jnp.where(owned, source_length[None, :], 0), axis=1)
    sent_rank = jnp.where(slot_j < sent_length, (sent_start + slot_j - 64 * l) % 256, -1)
    deliver = (sent_rank[:, None] == rows[None, :]).astype(jnp.float32)

    head = jnp.zeros((4, depth, quarter), jnp.float32)
    for s, piece in enumerate(pieces):
        head = lax.dynamic_update_slice(head, piece[None], ((x - s) % 4, 0, 0))
    head = lax.optimization_barrier(head.reshape(wide, quarter))

    leave = dot(hidden[64:], head)
    stay = lax.optimization_barrier(dot(hidden[:64], head))
    block = stay + shift_z(leave[:64], 1) + shift_z(leave[128:], -1) + shift_far(leave[64:128])
    logits = jnp.sum(swap(block.reshape(4, 16, quarter), "h"), axis=0)

    row_labels = lax.dynamic_slice(labels, (h * 16,), (16,))
    column = jnp.arange(quarter, dtype=jnp.int32) + j * columns + x * quarter
    onehot = (column[None, :] == row_labels[:, None]).astype(jnp.float32)
    peak = jnp.max(logits, axis=1)
    shifted = jnp.exp(logits - peak[:, None])
    stats = jnp.stack([peak, jnp.sum(shifted, axis=1), jnp.sum(logits * onehot, axis=1)], axis=0)
    stats = spread(stats, XYC, 32)
    row_peak = jnp.max(stats[:, 0], axis=0)
    exp_total = jnp.sum(stats[:, 1] * jnp.exp(stats[:, 0] - row_peak[None]), axis=0)
    logprobs = jnp.sum(stats[:, 2], axis=0) - row_peak - jnp.log(exp_total)
    scale = jnp.exp(peak - row_peak) / exp_total
    grad = onehot - shifted * scale[:, None]

    own = spread(grad, "h", 4).reshape(64, quarter)
    blocks = [own, shift_z(own, -1), shift_far(own), shift_z(own, 1)]
    grads = jnp.concatenate(blocks, axis=0)

    def sent(i):
        return dot(deliver[:, 64 * i : 64 * (i + 1)], dot(blocks[i], head, (1, 1), GRAD), (1, 0), GRAD)

    leaving = (sent(0) + sent(1) + sent(3) + sent(2)).reshape(32, 16, wide)
    summed = jnp.sum(swap(leaving, XYC), axis=0)

    grad_head = dot(hidden, grads, (0, 0), GRAD).reshape(4, depth, quarter)
    summed, grad_head_later = lax.optimization_barrier((summed, grad_head))

    def part(array, s):
        return lax.dynamic_index_in_dim(array, (x + s) % 4, 0, False)

    grad_weight = jnp.tile(part(grad_head_later, 0), (1, 4))
    for s in (1, 3, 2):
        grad_weight = lax.dynamic_update_slice(grad_weight, shift_x(part(grad_head, s), s), (0, (x - s) % 4 * quarter))

    parts = lax.dynamic_update_slice(jnp.zeros((16, META), jnp.float32), logprobs.reshape(4, 4), (h * 4, 0))
    parts = jnp.where(l == x, parts, 0.0)
    arrived = swap(jnp.concatenate([summed, parts], axis=1).reshape(16, 1, wide + META), Z)[:, 0]
    slot = arrived[:, :wide].reshape(16, 4, depth).transpose(1, 0, 2).reshape(width)
    grad_hidden = spread(slot, YC, 8)
    return jnp.sum(arrived[:, wide : wide + 4], axis=0), grad_hidden, grad_weight


def solution(mesh):
    grid = Mesh(mesh.devices.reshape(4, 4, 4, 4, 2), ("x", "h", "l", "y", "c"))
    dp = ("x", "h", "l")
    placed = (P(dp, None), P(dp, YC), P(dp), P(dp), P(dp))
    return jax.shard_map(
        on_device,
        mesh=grid,
        in_specs=placed,
        out_specs=(P(dp), P(dp, None), P(dp, YC)),
        check_vma=False,
    )
```

```python
import functools

import jax
import jax.numpy as jnp
from jax import lax
from jax.experimental import pallas as pl
from jax.experimental.pallas import tpu as pltpu
from jax.sharding import Mesh, PartitionSpec as P

HIGH = lax.Precision.HIGHEST
GRAD = lax.Precision.HIGH
Z = ("h", "l")
XYC = ("x", "y", "c")
YC = ("y", "c")
META = 128


def swap(blocks, axes):
    return lax.all_to_all(blocks, axes, split_axis=0, concat_axis=0, tiled=True)


def spread(block, axes, count):
    return swap(jnp.broadcast_to(block[None], (count, *block.shape)), axes)


def shift_z(block, step):
    return lax.ppermute(block, Z, [(i, (i + step) % 16) for i in range(16)])


def shift_far(block):
    pairs = [(2 * i + c, 2 * ((i + 2 - 4 * c) % 16) + c) for i in range(16) for c in range(2)]
    return lax.ppermute(block, ("h", "l", "c"), pairs)


def shift_x(block, step):
    return lax.ppermute(block, "x", [(i, (i + step) % 4) for i in range(4)])


def dot(a, b, contract=(1, 0), precision=HIGH):
    dims = (((contract[0],), (contract[1],)), ((), ()))
    return lax.dot_general(a, b, dims, precision=precision, preferred_element_type=jnp.float32)


def cut_kernel(quarter, weight, targets, lengths, owners, own, one, two, three, notes, target, sems):
    x = lax.axis_index("x")
    small = pltpu.make_async_copy(targets, target, sems.at[4])
    large = [
        pltpu.make_async_copy(
            weight.at[:, pl.ds(pl.multiple_of(lax.rem(x + s, 4) * quarter, 128), quarter)], block, sems.at[s]
        )
        for s, block in enumerate((own, one, two, three))
    ]
    small.start()
    for copy in large:
        copy.start()
    small.wait()
    lane = lax.broadcasted_iota(jnp.int32, (1, META), 1)
    values = [*(target[i] for i in range(8)), lengths[0], owners[0]]
    row = jnp.zeros((1, META), jnp.int32)
    for i, value in enumerate(values):
        row = jnp.where(lane == i, value, row)
    notes[...] = row.astype(jnp.float32)
    for copy in large:
        copy.wait()


def cut(weight, targets, lengths, owners):
    depth, columns = weight.shape
    quarter = columns // 4
    block = jax.ShapeDtypeStruct((depth, quarter), jnp.float32)
    anywhere = pl.BlockSpec(memory_space=pl.ANY)
    scalar = pl.BlockSpec(memory_space=pltpu.SMEM)
    return pl.pallas_call(
        functools.partial(cut_kernel, quarter),
        out_shape=(block, block, block, block, jax.ShapeDtypeStruct((1, META), jnp.float32)),
        in_specs=[anywhere, anywhere, scalar, scalar],
        out_specs=(*([anywhere] * 4), pl.BlockSpec(memory_space=pltpu.VMEM)),
        scratch_shapes=[
            pltpu.SMEM((8,), jnp.int32),
            pltpu.SemaphoreType.DMA((5,)),
        ],
        name="cut",
    )(weight, targets, lengths, owners)


def on_device(responses, weight, lengths, targets, owners):
    width = responses.shape[1]
    depth, columns = weight.shape
    quarter = columns // 4
    wide = 4 * depth
    x, h, l = lax.axis_index("x"), lax.axis_index("h"), lax.axis_index("l")
    j, c = lax.axis_index(YC), lax.axis_index("c")

    row = lax.dynamic_slice(responses, (j, 0), (1, width)).reshape(4, 16, depth)
    *blocks, notes = cut(weight, targets, lengths, owners)
    notes = jnp.broadcast_to(notes, (16, META))
    packed = jnp.concatenate([row.transpose(1, 0, 2).reshape(16, wide), notes], axis=1).reshape(1, 16, 1, wide + META)
    packed = jnp.broadcast_to(packed, (4, 16, 1, wide + META)).reshape(64, 1, wide + META)

    pieces = [blocks[0], *(shift_x(blocks[s], s) for s in range(1, 4))]
    mine = swap(packed, ("x", *Z)).reshape(64, wide + META)
    mine, pieces[0] = lax.optimization_barrier((mine, pieces[0]))

    slots = spread(mine, "y", 4).reshape(256, wide + META)
    _, pieces[3] = lax.optimization_barrier((slots, pieces[3]))
    slots_other = lax.ppermute(slots, "c", [(0, 1), (1, 0)])

    all_notes = slots[:, wide : wide + 10].astype(jnp.int32)
    source_length, source_owner = all_notes[:64, 8], all_notes[:64, 9]
    sources = jnp.arange(64, dtype=jnp.int32)

    def starts_of(source):
        return jnp.sum(jnp.where(sources[None, :] < source[:, None], source_length[None, :], 0), axis=1)

    rows = jnp.arange(256, dtype=jnp.int32)
    starts = starts_of(rows % 64)

    def chosen(core):
        slot_j = rows // 64 * 2 + core
        rank = jnp.where(slot_j < all_notes[:, 8], (starts + slot_j - 64 * l) % 256, -1)
        target = jnp.sum(jnp.where(jnp.arange(10)[None, :] == slot_j[:, None], all_notes, 0), axis=1)
        select = rank[None, :] == rows[:, None]
        return select.astype(jnp.float32), jnp.sum(jnp.where(select, target[None, :], 0), axis=1)

    select, labels = chosen(c)
    select_other, labels_other = chosen(1 - c)
    labels = labels + labels_other
    hidden = dot(select, slots[:, :wide]) + dot(select_other, slots_other[:, :wide])

    ids = jnp.arange(512, dtype=jnp.int32)
    slot_j = ids // 16 % 8
    owned = source_owner[None, :] == (ids // 128 * 16 + ids % 16)[:, None]
    sent_start = jnp.sum(jnp.where(owned, starts_of(sources)[None, :], 0), axis=1)
    sent_length = jnp.sum(jnp.where(owned, source_length[None, :], 0), axis=1)
    sent_rank = jnp.where(slot_j < sent_length, (sent_start + slot_j - 64 * l) % 256, -1)
    deliver = (sent_rank[:, None] == rows[None, :]).astype(jnp.float32)

    head = jnp.zeros((4, depth, quarter), jnp.float32)
    for s, piece in enumerate(pieces):
        head = lax.dynamic_update_slice(head, piece[None], ((x - s) % 4, 0, 0))
    head = lax.optimization_barrier(head.reshape(wide, quarter))

    leave = dot(hidden[64:], head)
    stay = lax.optimization_barrier(dot(hidden[:64], head))
    block = stay + shift_z(leave[:64], 1) + shift_z(leave[128:], -1) + shift_far(leave[64:128])
    logits = jnp.sum(swap(block.reshape(4, 16, quarter), "h"), axis=0)

    row_labels = lax.dynamic_slice(labels, (h * 16,), (16,))
    column = jnp.arange(quarter, dtype=jnp.int32) + j * columns + x * quarter
    onehot = (column[None, :] == row_labels[:, None]).astype(jnp.float32)
    peak = jnp.max(logits, axis=1)
    shifted = jnp.exp(logits - peak[:, None])
    stats = jnp.stack([peak, jnp.sum(shifted, axis=1), jnp.sum(logits * onehot, axis=1)], axis=0)
    stats = spread(stats, XYC, 32)
    row_peak = jnp.max(stats[:, 0], axis=0)
    exp_total = jnp.sum(stats[:, 1] * jnp.exp(stats[:, 0] - row_peak[None]), axis=0)
    logprobs = jnp.sum(stats[:, 2], axis=0) - row_peak - jnp.log(exp_total)
    scale = jnp.exp(peak - row_peak) / exp_total
    grad = onehot - shifted * scale[:, None]

    own = spread(grad, "h", 4).reshape(64, quarter)
    grads = jnp.concatenate([own, shift_z(own, -1), shift_far(own), shift_z(own, 1)], axis=0)

    grad_rows = dot(grads, head, (1, 1), GRAD)
    leaving = dot(deliver, grad_rows, (1, 0), GRAD).reshape(32, 16, wide)
    summed = jnp.sum(swap(leaving, XYC), axis=0)

    grad_head = dot(hidden, grads, (0, 0), GRAD).reshape(4, depth, quarter)
    summed, grad_head_later = lax.optimization_barrier((summed, grad_head))

    def part(array, s):
        return lax.dynamic_index_in_dim(array, (x + s) % 4, 0, False)

    grad_weight = jnp.tile(part(grad_head_later, 0), (1, 4))
    for s in (1, 3, 2):
        grad_weight = lax.dynamic_update_slice(grad_weight, shift_x(part(grad_head, s), s), (0, (x - s) % 4 * quarter))

    parts = lax.dynamic_update_slice(jnp.zeros((16, META), jnp.float32), logprobs.reshape(4, 4), (h * 4, 0))
    parts = jnp.where(l == x, parts, 0.0)
    arrived = swap(jnp.concatenate([summed, parts], axis=1).reshape(16, 1, wide + META), Z)[:, 0]
    slot = arrived[:, :wide].reshape(16, 4, depth).transpose(1, 0, 2).reshape(width)
    grad_hidden = spread(slot, YC, 8)
    return jnp.sum(arrived[:, wide : wide + 4], axis=0), grad_hidden, grad_weight


def solution(mesh):
    grid = Mesh(mesh.devices.reshape(4, 4, 4, 4, 2), ("x", "h", "l", "y", "c"))
    dp = ("x", "h", "l")
    placed = (P(dp, None), P(dp, YC), P(dp), P(dp), P(dp))
    return jax.shard_map(
        on_device,
        mesh=grid,
        in_specs=placed,
        out_specs=(P(dp), P(dp, None), P(dp, YC)),
        check_vma=False,
    )
```

```python
import jax
import jax.numpy as jnp
from jax import lax
from jax.sharding import Mesh, PartitionSpec as P

HIGH = lax.Precision.HIGHEST
GRAD = lax.Precision.HIGH
Z = ("h", "l")
XYC = ("x", "y", "c")
YC = ("y", "c")
META = 128


def swap(blocks, axes):
    return lax.all_to_all(blocks, axes, split_axis=0, concat_axis=0, tiled=True)


def spread(block, axes, count):
    return swap(jnp.broadcast_to(block[None], (count, *block.shape)), axes)


def shift_z(block, step):
    return lax.ppermute(block, Z, [(i, (i + step) % 16) for i in range(16)])


def shift_far(block):
    pairs = [(2 * i + c, 2 * ((i + 2 - 4 * c) % 16) + c) for i in range(16) for c in range(2)]
    return lax.ppermute(block, ("h", "l", "c"), pairs)


def shift_x(block, step):
    return lax.ppermute(block, "x", [(i, (i + step) % 4) for i in range(4)])


def dot(a, b, contract=(1, 0), precision=HIGH):
    dims = (((contract[0],), (contract[1],)), ((), ()))
    return lax.dot_general(a, b, dims, precision=precision, preferred_element_type=jnp.float32)


def on_device(responses, weight, lengths, targets, owners):
    width = responses.shape[1]
    depth, columns = weight.shape
    quarter = columns // 4
    wide = 4 * depth
    x, h, l = lax.axis_index("x"), lax.axis_index("h"), lax.axis_index("l")
    j, c = lax.axis_index(YC), lax.axis_index("c")

    row = lax.dynamic_slice(responses, (j, 0), (1, width)).reshape(4, 16, depth)
    notes = jnp.pad(jnp.concatenate([targets, lengths, owners]).astype(jnp.float32), (0, META - 10))
    notes = jnp.broadcast_to(notes, (16, META))
    packed = jnp.concatenate([row.transpose(1, 0, 2).reshape(16, wide), notes], axis=1).reshape(1, 16, 1, wide + META)
    packed = jnp.broadcast_to(packed, (4, 16, 1, wide + META)).reshape(64, 1, wide + META)

    def cut(s):
        return lax.dynamic_slice(weight, (0, (x + s) % 4 * quarter), (depth, quarter))

    pieces = [cut(0), *(shift_x(cut(s), s) for s in range(1, 4))]
    mine = swap(packed, ("x", *Z)).reshape(64, wide + META)
    mine, pieces[0] = lax.optimization_barrier((mine, pieces[0]))

    slots = spread(mine, "y", 4).reshape(256, wide + META)
    _, pieces[3] = lax.optimization_barrier((slots, pieces[3]))
    slots_other = lax.ppermute(slots, "c", [(0, 1), (1, 0)])

    all_notes = slots[:, wide : wide + 10].astype(jnp.int32)
    source_length, source_owner = all_notes[:64, 8], all_notes[:64, 9]
    sources = jnp.arange(64, dtype=jnp.int32)

    def starts_of(source):
        return jnp.sum(jnp.where(sources[None, :] < source[:, None], source_length[None, :], 0), axis=1)

    rows = jnp.arange(256, dtype=jnp.int32)
    starts = starts_of(rows % 64)

    def chosen(core):
        slot_j = rows // 64 * 2 + core
        rank = jnp.where(slot_j < all_notes[:, 8], (starts + slot_j - 64 * l) % 256, -1)
        target = jnp.sum(jnp.where(jnp.arange(10)[None, :] == slot_j[:, None], all_notes, 0), axis=1)
        select = rank[None, :] == rows[:, None]
        return select.astype(jnp.float32), jnp.sum(jnp.where(select, target[None, :], 0), axis=1)

    select, labels = chosen(c)
    select_other, labels_other = chosen(1 - c)
    labels = labels + labels_other
    hidden = dot(select, slots[:, :wide]) + dot(select_other, slots_other[:, :wide])

    ids = jnp.arange(512, dtype=jnp.int32)
    slot_j = ids // 16 % 8
    owned = source_owner[None, :] == (ids // 128 * 16 + ids % 16)[:, None]
    sent_start = jnp.sum(jnp.where(owned, starts_of(sources)[None, :], 0), axis=1)
    sent_length = jnp.sum(jnp.where(owned, source_length[None, :], 0), axis=1)
    sent_rank = jnp.where(slot_j < sent_length, (sent_start + slot_j - 64 * l) % 256, -1)
    deliver = (sent_rank[:, None] == rows[None, :]).astype(jnp.float32)

    head = jnp.zeros((4, depth, quarter), jnp.float32)
    for s, piece in enumerate(pieces):
        head = lax.dynamic_update_slice(head, piece[None], ((x - s) % 4, 0, 0))
    head = lax.optimization_barrier(head.reshape(wide, quarter))

    leave = dot(hidden[64:], head)
    stay = lax.optimization_barrier(dot(hidden[:64], head))
    block = stay + shift_z(leave[:64], 1) + shift_z(leave[128:], -1) + shift_far(leave[64:128])
    logits = jnp.sum(swap(block.reshape(4, 16, quarter), "h"), axis=0)

    row_labels = lax.dynamic_slice(labels, (h * 16,), (16,))
    column = jnp.arange(quarter, dtype=jnp.int32) + j * columns + x * quarter
    onehot = (column[None, :] == row_labels[:, None]).astype(jnp.float32)
    peak = jnp.max(logits, axis=1)
    shifted = jnp.exp(logits - peak[:, None])
    stats = jnp.stack([peak, jnp.sum(shifted, axis=1), jnp.sum(logits * onehot, axis=1)], axis=0)
    stats = spread(stats, XYC, 32)
    row_peak = jnp.max(stats[:, 0], axis=0)
    exp_total = jnp.sum(stats[:, 1] * jnp.exp(stats[:, 0] - row_peak[None]), axis=0)
    logprobs = jnp.sum(stats[:, 2], axis=0) - row_peak - jnp.log(exp_total)
    scale = jnp.exp(peak - row_peak) / exp_total
    grad = onehot - shifted * scale[:, None]

    own = spread(grad, "h", 4).reshape(64, quarter)
    grads = jnp.concatenate([own, shift_z(own, -1), shift_far(own), shift_z(own, 1)], axis=0)

    grad_rows = dot(grads, head, (1, 1), GRAD)
    leaving = dot(deliver, grad_rows, (1, 0), GRAD).reshape(32, 16, wide)
    summed = jnp.sum(swap(leaving, XYC), axis=0)

    grad_head = dot(hidden, grads, (0, 0), GRAD).reshape(4, depth, quarter)
    summed, grad_head_later = lax.optimization_barrier((summed, grad_head))

    def part(array, s):
        return lax.dynamic_index_in_dim(array, (x + s) % 4, 0, False)

    grad_weight = jnp.tile(part(grad_head_later, 0), (1, 4))
    for s in (1, 3, 2):
        grad_weight = lax.dynamic_update_slice(grad_weight, shift_x(part(grad_head, s), s), (0, (x - s) % 4 * quarter))

    parts = lax.dynamic_update_slice(jnp.zeros((16, META), jnp.float32), logprobs.reshape(4, 4), (h * 4, 0))
    parts = jnp.where(l == x, parts, 0.0)
    arrived = swap(jnp.concatenate([summed, parts], axis=1).reshape(16, 1, wide + META), Z)[:, 0]
    slot = arrived[:, :wide].reshape(16, 4, depth).transpose(1, 0, 2).reshape(width)
    grad_hidden = spread(slot, YC, 8)
    return jnp.sum(arrived[:, wide : wide + 4], axis=0), grad_hidden, grad_weight


def solution(mesh):
    grid = Mesh(mesh.devices.reshape(4, 4, 4, 4, 2), ("x", "h", "l", "y", "c"))
    dp = ("x", "h", "l")
    placed = (P(dp, None), P(dp, YC), P(dp), P(dp), P(dp))
    return jax.shard_map(
        on_device,
        mesh=grid,
        in_specs=placed,
        out_specs=(P(dp), P(dp, None), P(dp, YC)),
        check_vma=False,
    )
```

```python
import jax
import jax.numpy as jnp
from jax import lax
from jax.sharding import Mesh, PartitionSpec as P

HIGH = lax.Precision.HIGHEST
GRAD = lax.Precision.HIGH
Z = ("h", "l")
XYC = ("x", "y", "c")
YC = ("y", "c")
META = 128


def swap(blocks, axes):
    return lax.all_to_all(blocks, axes, split_axis=0, concat_axis=0, tiled=True)


def spread(block, axes, count):
    return swap(jnp.broadcast_to(block[None], (count, *block.shape)), axes)


def shift_z(block, step):
    return lax.ppermute(block, Z, [(i, (i + step) % 16) for i in range(16)])


def shift_far(block, sign):
    step = [2 * sign, -2 * sign]
    pairs = [(2 * i + c, 2 * ((i + step[c]) % 16) + c) for i in range(16) for c in range(2)]
    return lax.ppermute(block, ("h", "l", "c"), pairs)


def shift_x(block, step):
    return lax.ppermute(block, "x", [(i, (i + step) % 4) for i in range(4)])


def dot(a, b, contract=(1, 0), precision=HIGH):
    dims = (((contract[0],), (contract[1],)), ((), ()))
    return lax.dot_general(a, b, dims, precision=precision, preferred_element_type=jnp.float32)


def on_device(responses, weight, lengths, targets, owners):
    width = responses.shape[1]
    depth, columns = weight.shape
    quarter = columns // 4
    wide = 4 * depth
    x, h, l = lax.axis_index("x"), lax.axis_index("h"), lax.axis_index("l")
    j, c = lax.axis_index(YC), lax.axis_index("c")

    row = lax.dynamic_slice(responses, (j, 0), (1, width)).reshape(4, 16, depth)
    notes = jnp.pad(jnp.concatenate([targets, lengths, owners]).astype(jnp.float32), (0, META - 10))
    notes = jnp.broadcast_to(notes, (16, META))
    packed = jnp.concatenate([row.transpose(1, 0, 2).reshape(16, wide), notes], axis=1).reshape(1, 16, 1, wide + META)
    packed = jnp.broadcast_to(packed, (4, 16, 1, wide + META)).reshape(64, 1, wide + META)

    def cut(s):
        return lax.dynamic_slice(weight, (0, (x + s) % 4 * quarter), (depth, quarter))

    pieces = [cut(0), *(shift_x(cut(s), s) for s in range(1, 4))]
    mine = swap(packed, ("x", *Z)).reshape(64, wide + META)
    mine, pieces[0] = lax.optimization_barrier((mine, pieces[0]))

    slots = spread(mine, "y", 4).reshape(256, wide + META)
    _, pieces[3] = lax.optimization_barrier((slots, pieces[3]))
    slots_other = lax.ppermute(slots, "c", [(0, 1), (1, 0)])

    all_notes = slots[:, wide : wide + 10].astype(jnp.int32)
    source_length, source_owner = all_notes[:64, 8], all_notes[:64, 9]
    sources = jnp.arange(64, dtype=jnp.int32)

    def starts_of(source):
        return jnp.sum(jnp.where(sources[None, :] < source[:, None], source_length[None, :], 0), axis=1)

    def placed(rank):
        turn = (rank // 64 - l) % 4
        partner = h * 4 + l + jnp.where(turn == 3, -1, jnp.where((turn == 2) & (c == 1), -2, turn))
        group = (rank // 16 - partner % 16 // 4) % 4
        group = jnp.where((group == 1) | (group == 2), 3 - group, group)
        return turn * 64 + group * 16 + rank % 16

    rows = jnp.arange(256, dtype=jnp.int32)
    starts = starts_of(rows % 64)

    def chosen(core):
        slot_j = rows // 64 * 2 + core
        rank = jnp.where(slot_j < all_notes[:, 8], placed(starts + slot_j), -1)
        target = jnp.sum(jnp.where(jnp.arange(10)[None, :] == slot_j[:, None], all_notes, 0), axis=1)
        select = rank[None, :] == rows[:, None]
        return select.astype(jnp.float32), jnp.sum(jnp.where(select, target[None, :], 0), axis=1)

    select, labels = chosen(c)
    select_other, labels_other = chosen(1 - c)
    labels = labels + labels_other
    hidden = dot(select, slots[:, :wide]) + dot(select_other, slots_other[:, :wide])

    ids = jnp.arange(512, dtype=jnp.int32)
    slot_j = ids // 16 % 8
    owned = source_owner[None, :] == (ids // 128 * 16 + ids % 16)[:, None]
    sent_start = jnp.sum(jnp.where(owned, starts_of(sources)[None, :], 0), axis=1)
    sent_length = jnp.sum(jnp.where(owned, source_length[None, :], 0), axis=1)
    sent_rank = jnp.where(slot_j < sent_length, placed(sent_start + slot_j), -1)
    deliver = (sent_rank[:, None] == rows[None, :]).astype(jnp.float32)

    head = jnp.zeros((4, depth, quarter), jnp.float32)
    for s, piece in enumerate(pieces):
        head = lax.dynamic_update_slice(head, piece[None], ((x - s) % 4, 0, 0))
    head = lax.optimization_barrier(head.reshape(wide, quarter))

    leave = dot(hidden[64:], head)
    stay = lax.optimization_barrier(dot(hidden[:64], head))
    block = stay + shift_z(leave[:64], 1) + shift_z(leave[128:], -1) + shift_far(leave[64:128], 1)
    logits = block[:16] + shift_z(block[32:48], 4) + shift_z(block[48:], -4) + shift_z(block[16:32], 8)

    row_labels = labels[:16]
    column = jnp.arange(quarter, dtype=jnp.int32) + j * columns + x * quarter
    onehot = (column[None, :] == row_labels[:, None]).astype(jnp.float32)
    peak = jnp.max(logits, axis=1)
    shifted = jnp.exp(logits - peak[:, None])
    stats = jnp.stack([peak, jnp.sum(shifted, axis=1), jnp.sum(logits * onehot, axis=1)], axis=0)
    stats = spread(stats, XYC, 32)
    row_peak = jnp.max(stats[:, 0], axis=0)
    exp_total = jnp.sum(stats[:, 1] * jnp.exp(stats[:, 0] - row_peak[None]), axis=0)
    logprobs = jnp.sum(stats[:, 2], axis=0) - row_peak - jnp.log(exp_total)
    scale = jnp.exp(peak - row_peak) / exp_total
    grad = onehot - shifted * scale[:, None]

    own = jnp.concatenate([grad, shift_z(grad, 8), shift_z(grad, -4), shift_z(grad, 4)], axis=0)
    grads = jnp.concatenate([own, shift_z(own, -1), shift_far(own, -1), shift_z(own, 1)], axis=0)

    grad_rows = dot(grads, head, (1, 1), GRAD)
    leaving = dot(deliver, grad_rows, (1, 0), GRAD).reshape(32, 16, wide)
    summed = jnp.sum(swap(leaving, XYC), axis=0)

    grad_head = dot(hidden, grads, (0, 0), GRAD).reshape(4, depth, quarter)
    summed, grad_head_later = lax.optimization_barrier((summed, grad_head))

    def part(array, s):
        return lax.dynamic_index_in_dim(array, (x + s) % 4, 0, False)

    grad_weight = jnp.tile(part(grad_head_later, 0), (1, 4))
    for s in (1, 3, 2):
        grad_weight = lax.dynamic_update_slice(grad_weight, shift_x(part(grad_head, s), s), (0, (x - s) % 4 * quarter))

    parts = lax.dynamic_update_slice(jnp.zeros((16, META), jnp.float32), logprobs.reshape(4, 4), (h * 4, 0))
    parts = jnp.where(l == x, parts, 0.0)
    arrived = swap(jnp.concatenate([summed, parts], axis=1).reshape(16, 1, wide + META), Z)[:, 0]
    slot = arrived[:, :wide].reshape(16, 4, depth).transpose(1, 0, 2).reshape(width)
    grad_hidden = spread(slot, YC, 8)
    return jnp.sum(arrived[:, wide : wide + 4], axis=0), grad_hidden, grad_weight


def solution(mesh):
    grid = Mesh(mesh.devices.reshape(4, 4, 4, 4, 2), ("x", "h", "l", "y", "c"))
    dp = ("x", "h", "l")
    placed = (P(dp, None), P(dp, YC), P(dp), P(dp), P(dp))
    return jax.shard_map(
        on_device,
        mesh=grid,
        in_specs=placed,
        out_specs=(P(dp), P(dp, None), P(dp, YC)),
        check_vma=False,
    )
```

```python
import jax
import jax.numpy as jnp
from jax import lax
from jax.sharding import Mesh, PartitionSpec as P

HIGH = lax.Precision.HIGHEST
GRAD = lax.Precision.HIGH
Z = ("h", "l")
XYC = ("x", "y", "c")
YC = ("y", "c")
META = 128


def swap(blocks, axes):
    return lax.all_to_all(blocks, axes, split_axis=0, concat_axis=0, tiled=True)


def spread(block, axes, count):
    return swap(jnp.broadcast_to(block[None], (count, *block.shape)), axes)


def shift_z(block, step):
    return lax.ppermute(block, Z, [(i, (i + step) % 16) for i in range(16)])


def shift_far(block):
    pairs = [(2 * i + c, 2 * ((i + 2 - 4 * c) % 16) + c) for i in range(16) for c in range(2)]
    return lax.ppermute(block, ("h", "l", "c"), pairs)


def shift_x(block, step):
    return lax.ppermute(block, "x", [(i, (i + step) % 4) for i in range(4)])


def dot(a, b, contract=(1, 0), precision=HIGH):
    dims = (((contract[0],), (contract[1],)), ((), ()))
    return lax.dot_general(a, b, dims, precision=precision, preferred_element_type=jnp.float32)


def on_device(responses, weight, lengths, targets, owners):
    width = responses.shape[1]
    depth, columns = weight.shape
    quarter = columns // 4
    wide = 4 * depth
    x, h, l = lax.axis_index("x"), lax.axis_index("h"), lax.axis_index("l")
    j, c = lax.axis_index(YC), lax.axis_index("c")

    row = lax.dynamic_slice(responses, (j, 0), (1, width)).reshape(4, 16, depth)
    notes = jnp.pad(targets, (0, META - 8)) + jnp.pad(lengths, (8, META - 9)) + jnp.pad(owners, (9, META - 10))
    notes = notes.astype(jnp.float32)
    notes = jnp.broadcast_to(notes, (16, META))
    packed = jnp.concatenate([row.transpose(1, 0, 2).reshape(16, wide), notes], axis=1).reshape(1, 16, 1, wide + META)
    packed = jnp.broadcast_to(packed, (4, 16, 1, wide + META)).reshape(64, 1, wide + META)

    def cut(s):
        return lax.dynamic_slice(weight, (0, (x + s) % 4 * quarter), (depth, quarter))

    pieces = [cut(0), *(shift_x(cut(s), s) for s in range(1, 4))]
    mine = swap(packed, ("x", *Z)).reshape(64, wide + META)
    mine, pieces[0] = lax.optimization_barrier((mine, pieces[0]))

    slots = spread(mine, "y", 4).reshape(256, wide + META)
    _, pieces[3] = lax.optimization_barrier((slots, pieces[3]))
    slots_other = lax.ppermute(slots, "c", [(0, 1), (1, 0)])

    all_notes = slots[:, wide : wide + 10].astype(jnp.int32)
    source_length, source_owner = all_notes[:64, 8], all_notes[:64, 9]
    sources = jnp.arange(64, dtype=jnp.int32)

    def starts_of(source):
        return jnp.sum(jnp.where(sources[None, :] < source[:, None], source_length[None, :], 0), axis=1)

    rows = jnp.arange(256, dtype=jnp.int32)
    starts = starts_of(rows % 64)

    def chosen(core):
        slot_j = rows // 64 * 2 + core
        rank = jnp.where(slot_j < all_notes[:, 8], (starts + slot_j - 64 * l) % 256, -1)
        target = jnp.sum(jnp.where(jnp.arange(10)[None, :] == slot_j[:, None], all_notes, 0), axis=1)
        select = rank[None, :] == rows[:, None]
        return select.astype(jnp.float32), jnp.sum(jnp.where(select, target[None, :], 0), axis=1)

    select, labels = chosen(c)
    select_other, labels_other = chosen(1 - c)
    labels = labels + labels_other
    hidden = dot(select, slots[:, :wide]) + dot(select_other, slots_other[:, :wide])

    ids = jnp.arange(512, dtype=jnp.int32)
    slot_j = ids // 16 % 8
    owned = source_owner[None, :] == (ids // 128 * 16 + ids % 16)[:, None]
    sent_start = jnp.sum(jnp.where(owned, starts_of(sources)[None, :], 0), axis=1)
    sent_length = jnp.sum(jnp.where(owned, source_length[None, :], 0), axis=1)
    sent_rank = jnp.where(slot_j < sent_length, (sent_start + slot_j - 64 * l) % 256, -1)
    deliver = (sent_rank[:, None] == rows[None, :]).astype(jnp.float32)

    head = jnp.zeros((4, depth, quarter), jnp.float32)
    for s, piece in enumerate(pieces):
        head = lax.dynamic_update_slice(head, piece[None], ((x - s) % 4, 0, 0))
    head = lax.optimization_barrier(head.reshape(wide, quarter))

    leave = dot(hidden[64:], head)
    stay = lax.optimization_barrier(dot(hidden[:64], head))
    block = stay + shift_z(leave[:64], 1) + shift_z(leave[128:], -1) + shift_far(leave[64:128])
    logits = jnp.sum(swap(block.reshape(4, 16, quarter), "h"), axis=0)

    row_labels = lax.dynamic_slice(labels, (h * 16,), (16,))
    column = jnp.arange(quarter, dtype=jnp.int32) + j * columns + x * quarter
    onehot = (column[None, :] == row_labels[:, None]).astype(jnp.float32)
    peak = jnp.max(logits, axis=1)
    shifted = jnp.exp(logits - peak[:, None])
    stats = jnp.stack([peak, jnp.sum(shifted, axis=1), jnp.sum(logits * onehot, axis=1)], axis=0)
    stats = spread(stats, XYC, 32)
    row_peak = jnp.max(stats[:, 0], axis=0)
    exp_total = jnp.sum(stats[:, 1] * jnp.exp(stats[:, 0] - row_peak[None]), axis=0)
    logprobs = jnp.sum(stats[:, 2], axis=0) - row_peak - jnp.log(exp_total)
    scale = jnp.exp(peak - row_peak) / exp_total
    grad = onehot - shifted * scale[:, None]

    own = spread(grad, "h", 4).reshape(64, quarter)
    grads = jnp.concatenate([own, shift_z(own, -1), shift_far(own), shift_z(own, 1)], axis=0)

    grad_rows = dot(grads, head, (1, 1))
    leaving = dot(deliver, grad_rows, (1, 0), GRAD).reshape(32, 16, wide)
    summed = jnp.sum(swap(leaving, XYC), axis=0)

    grad_head = dot(hidden, grads, (0, 0), GRAD).reshape(4, depth, quarter)
    summed, grad_head_later = lax.optimization_barrier((summed, grad_head))

    def part(array, s):
        return lax.dynamic_index_in_dim(array, (x + s) % 4, 0, False)

    grad_weight = jnp.tile(part(grad_head_later, 0), (1, 4))
    for s in (1, 3, 2):
        grad_weight = lax.dynamic_update_slice(grad_weight, shift_x(part(grad_head, s), s), (0, (x - s) % 4 * quarter))

    parts = lax.dynamic_update_slice(jnp.zeros((16, META), jnp.float32), logprobs.reshape(4, 4), (h * 4, 0))
    parts = jnp.where(l == x, parts, 0.0)
    arrived = swap(jnp.concatenate([summed, parts], axis=1).reshape(16, 1, wide + META), Z)[:, 0]
    slot = arrived[:, :wide].reshape(16, 4, depth).transpose(1, 0, 2).reshape(width)
    grad_hidden = spread(slot, YC, 8)
    return jnp.sum(arrived[:, wide : wide + 4], axis=0), grad_hidden, grad_weight


def solution(mesh):
    grid = Mesh(mesh.devices.reshape(4, 4, 4, 4, 2), ("x", "h", "l", "y", "c"))
    dp = ("x", "h", "l")
    placed = (P(dp, None), P(dp, YC), P(dp), P(dp), P(dp))
    return jax.shard_map(
        on_device,
        mesh=grid,
        in_specs=placed,
        out_specs=(P(dp), P(dp, None), P(dp, YC)),
        check_vma=False,
    )
```

```python
import jax
import jax.numpy as jnp
from jax import lax
from jax.sharding import Mesh, PartitionSpec as P

HIGH = lax.Precision.HIGHEST
GRAD = lax.Precision.HIGH
Z = ("h", "l")
XYC = ("x", "y", "c")
YC = ("y", "c")
META = 128


def swap(blocks, axes):
    return lax.all_to_all(blocks, axes, split_axis=0, concat_axis=0, tiled=True)


def spread(block, axes, count):
    return swap(jnp.broadcast_to(block[None], (count, *block.shape)), axes)


def shift_z(block, step):
    return lax.ppermute(block, Z, [(i, (i + step) % 16) for i in range(16)])


def shift_far(block):
    pairs = [(2 * i + c, 2 * ((i + 2 - 4 * c) % 16) + c) for i in range(16) for c in range(2)]
    return lax.ppermute(block, ("h", "l", "c"), pairs)


def shift_x(block, step):
    return lax.ppermute(block, "x", [(i, (i + step) % 4) for i in range(4)])


def dot(a, b, contract=(1, 0), precision=HIGH):
    dims = (((contract[0],), (contract[1],)), ((), ()))
    return lax.dot_general(a, b, dims, precision=precision, preferred_element_type=jnp.float32)


def on_device(responses, weight, lengths, targets, owners):
    width = responses.shape[1]
    depth, columns = weight.shape
    quarter = columns // 4
    wide = 4 * depth
    x, h, l = lax.axis_index("x"), lax.axis_index("h"), lax.axis_index("l")
    j, c = lax.axis_index(YC), lax.axis_index("c")

    row = lax.dynamic_slice(responses, (j, 0), (1, width)).reshape(4, 16, depth)
    notes = jnp.pad(targets, (0, META - 8)) + jnp.pad(lengths, (8, META - 9)) + jnp.pad(owners, (9, META - 10))
    notes = notes.astype(jnp.float32)
    notes = jnp.broadcast_to(notes, (16, META))
    packed = jnp.concatenate([row.transpose(1, 0, 2).reshape(16, wide), notes], axis=1).reshape(1, 16, 1, wide + META)
    packed = jnp.broadcast_to(packed, (4, 16, 1, wide + META)).reshape(64, 1, wide + META)

    def cut(s):
        return lax.dynamic_slice(weight, (0, (x + s) % 4 * quarter), (depth, quarter))

    pieces = [cut(0), *(shift_x(cut(s), s) for s in range(1, 4))]
    mine = swap(packed, ("x", *Z)).reshape(64, wide + META)
    mine, pieces[0] = lax.optimization_barrier((mine, pieces[0]))

    slots = spread(mine, "y", 4).reshape(256, wide + META)
    _, pieces[3] = lax.optimization_barrier((slots, pieces[3]))
    slots_other = lax.ppermute(slots, "c", [(0, 1), (1, 0)])

    all_notes = slots[:, wide : wide + 10].astype(jnp.int32)
    source_length, source_owner = all_notes[:64, 8], all_notes[:64, 9]
    sources = jnp.arange(64, dtype=jnp.int32)

    def starts_of(source):
        return jnp.sum(jnp.where(sources[None, :] < source[:, None], source_length[None, :], 0), axis=1)

    rows = jnp.arange(256, dtype=jnp.int32)
    starts = starts_of(rows % 64)

    def chosen(core):
        slot_j = rows // 64 * 2 + core
        rank = jnp.where(slot_j < all_notes[:, 8], (starts + slot_j - 64 * l) % 256, -1)
        target = jnp.sum(jnp.where(jnp.arange(10)[None, :] == slot_j[:, None], all_notes, 0), axis=1)
        select = rank[None, :] == rows[:, None]
        return select.astype(jnp.float32), jnp.sum(jnp.where(select, target[None, :], 0), axis=1)

    select, labels = chosen(c)
    select_other, labels_other = chosen(1 - c)
    labels = labels + labels_other
    hidden = dot(select, slots[:, :wide]) + dot(select_other, slots_other[:, :wide])

    ids = jnp.arange(512, dtype=jnp.int32)
    slot_j = ids // 16 % 8
    owned = source_owner[None, :] == (ids // 128 * 16 + ids % 16)[:, None]
    sent_start = jnp.sum(jnp.where(owned, starts_of(sources)[None, :], 0), axis=1)
    sent_length = jnp.sum(jnp.where(owned, source_length[None, :], 0), axis=1)
    sent_rank = jnp.where(slot_j < sent_length, (sent_start + slot_j - 64 * l) % 256, -1)
    deliver = (sent_rank[:, None] == rows[None, :]).astype(jnp.float32)

    head = jnp.zeros((4, depth, quarter), jnp.float32)
    for s, piece in enumerate(pieces):
        head = lax.dynamic_update_slice(head, piece[None], ((x - s) % 4, 0, 0))
    head = lax.optimization_barrier(head.reshape(wide, quarter))

    leave = dot(hidden[64:], head)
    stay = lax.optimization_barrier(dot(hidden[:64], head))
    block = stay + shift_z(leave[:64], 1) + shift_z(leave[128:], -1) + shift_far(leave[64:128])

    def group(s):
        return lax.dynamic_slice(block, ((h + s) % 4 * 16, 0), (16, quarter))

    logits = group(0) + shift_z(group(1), 4) + shift_z(group(3), -4) + shift_z(group(2), 8)

    row_labels = lax.dynamic_slice(labels, (h * 16,), (16,))
    column = jnp.arange(quarter, dtype=jnp.int32) + j * columns + x * quarter
    onehot = (column[None, :] == row_labels[:, None]).astype(jnp.float32)
    peak = jnp.max(logits, axis=1)
    shifted = jnp.exp(logits - peak[:, None])
    stats = jnp.stack([peak, jnp.sum(shifted, axis=1), jnp.sum(logits * onehot, axis=1)], axis=0)
    stats = spread(stats, XYC, 32)
    row_peak = jnp.max(stats[:, 0], axis=0)
    exp_total = jnp.sum(stats[:, 1] * jnp.exp(stats[:, 0] - row_peak[None]), axis=0)
    logprobs = jnp.sum(stats[:, 2], axis=0) - row_peak - jnp.log(exp_total)
    scale = jnp.exp(peak - row_peak) / exp_total
    grad = onehot - shifted * scale[:, None]

    own = spread(grad, "h", 4).reshape(64, quarter)
    grads = jnp.concatenate([own, shift_z(own, -1), shift_far(own), shift_z(own, 1)], axis=0)

    grad_rows = dot(grads, head, (1, 1))
    leaving = dot(deliver, grad_rows, (1, 0), GRAD).reshape(32, 16, wide)
    summed = jnp.sum(swap(leaving, XYC), axis=0)

    grad_head = dot(hidden, grads, (0, 0), GRAD).reshape(4, depth, quarter)
    summed, grad_head_later = lax.optimization_barrier((summed, grad_head))

    def part(array, s):
        return lax.dynamic_index_in_dim(array, (x + s) % 4, 0, False)

    grad_weight = jnp.tile(part(grad_head_later, 0), (1, 4))
    for s in (1, 3, 2):
        grad_weight = lax.dynamic_update_slice(grad_weight, shift_x(part(grad_head, s), s), (0, (x - s) % 4 * quarter))

    parts = lax.dynamic_update_slice(jnp.zeros((16, META), jnp.float32), logprobs.reshape(4, 4), (h * 4, 0))
    parts = jnp.where(l == x, parts, 0.0)
    arrived = swap(jnp.concatenate([summed, parts], axis=1).reshape(16, 1, wide + META), Z)[:, 0]
    slot = arrived[:, :wide].reshape(16, 4, depth).transpose(1, 0, 2).reshape(width)
    grad_hidden = spread(slot, YC, 8)
    return jnp.sum(arrived[:, wide : wide + 4], axis=0), grad_hidden, grad_weight


def solution(mesh):
    grid = Mesh(mesh.devices.reshape(4, 4, 4, 4, 2), ("x", "h", "l", "y", "c"))
    dp = ("x", "h", "l")
    placed = (P(dp, None), P(dp, YC), P(dp), P(dp), P(dp))
    return jax.shard_map(
        on_device,
        mesh=grid,
        in_specs=placed,
        out_specs=(P(dp), P(dp, None), P(dp, YC)),
        check_vma=False,
    )
```

```python
import jax
import jax.numpy as jnp
from jax import lax
from jax.sharding import Mesh, PartitionSpec as P

HIGH = lax.Precision.HIGHEST
GRAD = lax.Precision.HIGH
Z = ("h", "l")
XYC = ("x", "y", "c")
YC = ("y", "c")
META = 128


def swap(blocks, axes):
    return lax.all_to_all(blocks, axes, split_axis=0, concat_axis=0, tiled=True)


def spread(block, axes, count):
    return swap(jnp.broadcast_to(block[None], (count, *block.shape)), axes)


def shift_z(block, step):
    return lax.ppermute(block, Z, [(i, (i + step) % 16) for i in range(16)])


def shift_far(block):
    pairs = [(2 * i + c, 2 * ((i + 2 - 4 * c) % 16) + c) for i in range(16) for c in range(2)]
    return lax.ppermute(block, ("h", "l", "c"), pairs)


def shift_x(block, step):
    return lax.ppermute(block, "x", [(i, (i + step) % 4) for i in range(4)])


def dot(a, b, contract=(1, 0), precision=HIGH):
    dims = (((contract[0],), (contract[1],)), ((), ()))
    return lax.dot_general(a, b, dims, precision=precision, preferred_element_type=jnp.float32)


def on_device(responses, weight, lengths, targets, owners):
    width = responses.shape[1]
    depth, columns = weight.shape
    quarter = columns // 4
    wide = 4 * depth
    x, h, l = lax.axis_index("x"), lax.axis_index("h"), lax.axis_index("l")
    j, c = lax.axis_index(YC), lax.axis_index("c")

    row = lax.dynamic_slice(responses, (j, 0), (1, width)).reshape(4, 16, depth)
    notes = jnp.pad(targets, (0, META - 8)) + jnp.pad(lengths, (8, META - 9)) + jnp.pad(owners, (9, META - 10))
    notes = notes.astype(jnp.float32)
    notes = jnp.broadcast_to(notes, (16, META))
    packed = jnp.concatenate([row.transpose(1, 0, 2).reshape(16, wide), notes], axis=1).reshape(1, 16, 1, wide + META)
    packed = jnp.broadcast_to(packed, (4, 16, 1, wide + META)).reshape(64, 1, wide + META)

    def cut(s):
        return lax.dynamic_slice(weight, (0, (x + s) % 4 * quarter), (depth, quarter))

    pieces = [cut(0), *(shift_x(cut(s), s) for s in range(1, 4))]
    mine = swap(packed, ("x", *Z)).reshape(64, wide + META)
    mine, pieces[0] = lax.optimization_barrier((mine, pieces[0]))

    slots = spread(mine, "y", 4).reshape(256, wide + META)
    _, pieces[3] = lax.optimization_barrier((slots, pieces[3]))
    slots_other = lax.ppermute(slots, "c", [(0, 1), (1, 0)])

    all_notes = slots[:, wide : wide + 10].astype(jnp.int32)
    source_length, source_owner = all_notes[:64, 8], all_notes[:64, 9]
    sources = jnp.arange(64, dtype=jnp.int32)

    def starts_of(source):
        return jnp.sum(jnp.where(sources[None, :] < source[:, None], source_length[None, :], 0), axis=1)

    rows = jnp.arange(256, dtype=jnp.int32)
    starts = starts_of(rows % 64)

    def chosen(core):
        slot_j = rows // 64 * 2 + core
        rank = jnp.where(slot_j < all_notes[:, 8], (starts + slot_j - 64 * l) % 256, -1)
        target = jnp.sum(jnp.where(jnp.arange(10)[None, :] == slot_j[:, None], all_notes, 0), axis=1)
        select = rank[None, :] == rows[:, None]
        return select.astype(jnp.float32), jnp.sum(jnp.where(select, target[None, :], 0), axis=1)

    select, labels = chosen(c)
    select_other, labels_other = chosen(1 - c)
    labels = labels + labels_other
    hidden = dot(select, slots[:, :wide]) + dot(select_other, slots_other[:, :wide])

    ids = jnp.arange(512, dtype=jnp.int32)
    slot_j = ids // 16 % 8
    owned = source_owner[None, :] == (ids // 128 * 16 + ids % 16)[:, None]
    sent_start = jnp.sum(jnp.where(owned, starts_of(sources)[None, :], 0), axis=1)
    sent_length = jnp.sum(jnp.where(owned, source_length[None, :], 0), axis=1)
    sent_rank = jnp.where(slot_j < sent_length, (sent_start + slot_j - 64 * l) % 256, -1)
    deliver = (sent_rank[:, None] == rows[None, :]).astype(jnp.float32)

    head = jnp.zeros((4, depth, quarter), jnp.float32)
    for s, piece in enumerate(pieces):
        head = lax.dynamic_update_slice(head, piece[None], ((x - s) % 4, 0, 0))
    head = lax.optimization_barrier(head.reshape(wide, quarter))

    leave = dot(hidden[64:], head)
    stay = lax.optimization_barrier(dot(hidden[:64], head))
    block = stay + shift_z(leave[:64], 1) + shift_z(leave[128:], -1) + shift_far(leave[64:128])
    logits = jnp.sum(swap(block.reshape(4, 16, quarter), "h"), axis=0)

    row_labels = lax.dynamic_slice(labels, (h * 16,), (16,))
    column = jnp.arange(quarter, dtype=jnp.int32) + j * columns + x * quarter
    onehot = (column[None, :] == row_labels[:, None]).astype(jnp.float32)
    peak = jnp.max(logits, axis=1)
    shifted = jnp.exp(logits - peak[:, None])
    stats = jnp.stack([peak, jnp.sum(shifted, axis=1), jnp.sum(logits * onehot, axis=1)], axis=0)
    stats = spread(stats, XYC, 32)
    row_peak = jnp.max(stats[:, 0], axis=0)
    exp_total = jnp.sum(stats[:, 1] * jnp.exp(stats[:, 0] - row_peak[None]), axis=0)
    logprobs = jnp.sum(stats[:, 2], axis=0) - row_peak - jnp.log(exp_total)
    scale = jnp.exp(peak - row_peak) / exp_total
    grad = onehot - shifted * scale[:, None]

    own = spread(grad, "h", 4).reshape(64, quarter)
    after, far, ahead = shift_z(own, -1), shift_far(own), shift_z(own, 1)
    grads = jnp.concatenate([own, after, far, ahead], axis=0)

    early = lax.optimization_barrier(dot(jnp.concatenate([own, far, ahead], axis=0), head, (1, 1)))
    grad_rows = jnp.concatenate([early[:64], dot(after, head, (1, 1)), early[64:]], axis=0)
    leaving = dot(deliver, grad_rows, (1, 0), GRAD).reshape(32, 16, wide)
    summed = jnp.sum(swap(leaving, XYC), axis=0)

    grad_head = dot(hidden, grads, (0, 0), GRAD).reshape(4, depth, quarter)
    summed, grad_head_later = lax.optimization_barrier((summed, grad_head))

    def part(array, s):
        return lax.dynamic_index_in_dim(array, (x + s) % 4, 0, False)

    grad_weight = jnp.tile(part(grad_head_later, 0), (1, 4))
    for s in (1, 3, 2):
        grad_weight = lax.dynamic_update_slice(grad_weight, shift_x(part(grad_head, s), s), (0, (x - s) % 4 * quarter))

    parts = lax.dynamic_update_slice(jnp.zeros((16, META), jnp.float32), logprobs.reshape(4, 4), (h * 4, 0))
    parts = jnp.where(l == x, parts, 0.0)
    arrived = swap(jnp.concatenate([summed, parts], axis=1).reshape(16, 1, wide + META), Z)[:, 0]
    slot = arrived[:, :wide].reshape(16, 4, depth).transpose(1, 0, 2).reshape(width)
    grad_hidden = spread(slot, YC, 8)
    return jnp.sum(arrived[:, wide : wide + 4], axis=0), grad_hidden, grad_weight


def solution(mesh):
    grid = Mesh(mesh.devices.reshape(4, 4, 4, 4, 2), ("x", "h", "l", "y", "c"))
    dp = ("x", "h", "l")
    placed = (P(dp, None), P(dp, YC), P(dp), P(dp), P(dp))
    return jax.shard_map(
        on_device,
        mesh=grid,
        in_specs=placed,
        out_specs=(P(dp), P(dp, None), P(dp, YC)),
        check_vma=False,
    )
```
